256 devices in a mesh: seq: 32 (over y, z), head: 8 (over x, core).
Axes of the slice: x: 4, y: 4, z: 8, core: 2. Of those that a mesh axis runs over, the one named last changes fastest.
Arguments:
- tokens: bfloat16 [16384, 2048], P('seq'), may hold values from -12 to 12
- w_qkv: bfloat16 [3, 2048, 2048], P(None, None, 'head'), may hold values from -1 to 1
- w_out: bfloat16 [2048, 2048], P('head'), may hold values from -1.5 to 1.5
- offsets: int32 [16], P('head'), may hold values from 0 to 7
- cotangent: bfloat16 [16384, 2048], P('seq'), may hold values from -6 to 6
Outputs:
- output: bfloat16 [16384, 2048], P('seq', 'head')
- input_grad: bfloat16 [16384, 2048], P('seq', 'head')
The draws below stay inside these ranges and needn't reach their ends.
All inputs are finite; a program needn't handle non-finite values.
Results may differ from the reference program's by a relative error of at most 0.025.
Values may be sent and summed in bfloat16 or wider, within the bound.
A program may use at most 64 MiB of HBM per device.

```python
import math
import jax
import jax.numpy as jnp
from jax import lax

D = 2048
HEADS = 16
HD = 128
LEVELS = 4
TOK_DEV = 512
TOKENS = 16384
HEADS_DEV = 2
N_HEAD = 8


def draw_tokens(key, part):
    key = jax.random.fold_in(key, 101)
    first = jax.random.fold_in(key, 0)
    return jax.random.truncated_normal(first, -6.0, 6.0, (TOKENS, D), jnp.float32).astype(jnp.bfloat16)


def draw_w_qkv(key, part):
    key = jax.random.fold_in(key, 202)
    first = jax.random.fold_in(key, 0)
    base = jax.random.truncated_normal(first, -4.0, 4.0, (3, D, D), jnp.float32) / math.sqrt(D)
    return base.astype(jnp.bfloat16)


def with_ends(array, rng, low, high):
    longest = array.shape.index(max(array.shape))
    spots = []
    for shift in (0, 1):
        where = [jax.random.randint(jax.random.fold_in(rng, axis), (), 0, length) for axis, length in enumerate(array.shape)]
        where[longest] = (where[longest] + shift) % array.shape[longest]
        spots.append(tuple(where))
    return array.at[spots[0]].set(low).at[spots[1]].set(high)


def block_scale(own_key, extent, cuts, smallest, top_value):
    gain = 1.0
    for dim, blocks in cuts:
        draws = jax.random.uniform(jax.random.fold_in(jax.random.fold_in(own_key, 6), dim), (blocks,), jnp.float32, smallest / len(cuts), top_value / len(cuts))
        gain = gain * jnp.repeat(jnp.exp(draws), extent[dim] // blocks).reshape((-1,) + (1,) * (len(extent) - 1 - dim))
    return gain


def bell_draw(key, dims, deviation, bound, cuts=(), held_as=jnp.bfloat16):
    result = deviation * jax.random.normal(key, dims, jnp.float32)
    if cuts:
        result = result * block_scale(key, dims, cuts, -0.22, 0.18)
    return jnp.clip(result, -bound, bound).astype(held_as)


def setup_inputs(seed: int = 0) -> dict:
    splits = jax.random.split(jax.random.key(seed), 6)
    tokens = draw_tokens(jax.random.fold_in(splits[5], 71), 0)
    w_qkv = draw_w_qkv(jax.random.fold_in(splits[5], 71), 0)
    w_out = bell_draw(splits[2], (D, D), HEADS ** -0.5, 1.5, ((0, 8),))
    offsets = with_ends(jax.random.randint(splits[3], (HEADS,), 0, 2 ** (LEVELS - 1)), jax.random.fold_in(splits[3], 1), 0, (2 ** (LEVELS - 1)) - 1).astype(jnp.int32)
    cotangent = bell_draw(splits[4], (TOKENS, D), 1.0, 6.0, ((0, 32),))
    return {"tokens": tokens, "w_qkv": w_qkv, "w_out": w_out, "offsets": offsets, "cotangent": cotangent}


def lowered(values):
    return lax.optimization_barrier(values.astype(jnp.bfloat16))

def taken(values, level_k, phase):
    stride = 2 ** level_k
    shaped = values.reshape((TOKENS // (TOK_DEV * stride), TOK_DEV, stride) + values.shape[1:])
    return lax.dynamic_index_in_dim(shaped, phase, axis=2, keepdims=False)

def placed(values, level_k, phase, fill):
    stride = 2 ** level_k
    lanes = jnp.arange(stride, dtype=jnp.int32) == phase
    extra = (1,) * (values.ndim - 2)
    wide = jnp.where(lanes.reshape((1, 1, stride) + extra), values[:, :, None], fill)
    return wide.reshape((TOKENS,) + values.shape[2:])

def batched(form, left, right):
    return jnp.einsum(form, left.astype(jnp.float32), right.astype(jnp.float32), precision=lax.Precision.HIGHEST)

def one_head(tokens, cotangent, w_query, w_key, w_value, w_output, phase_all):
    scaling = 1.0 / math.sqrt(HD)
    queries = lowered(jnp.dot(tokens, w_query, preferred_element_type=jnp.float32) * scaling).astype(jnp.float32)
    keys = lowered(jnp.dot(tokens, w_key, preferred_element_type=jnp.float32)).astype(jnp.float32)
    values = lowered(jnp.dot(tokens, w_value, preferred_element_type=jnp.float32)).astype(jnp.float32)
    phases = [(phase_all % 2 ** level_k).astype(jnp.int32) for level_k in range(LEVELS)]
    query_list, key_list, value_list, score_list = ([], [], [], [])
    top = jnp.full((TOKENS,), -jnp.inf, jnp.float32)
    for level_k in range(LEVELS):
        phase = phases[level_k]
        query_taken = taken(queries, level_k, phase)
        key_taken = taken(keys, level_k, phase)
        value_taken = taken(values, level_k, phase)
        scores = batched('nqd,nkd->nqk', query_taken, key_taken)
        query_list.append(query_taken)
        key_list.append(key_taken)
        value_list.append(value_taken)
        score_list.append(scores)
        top = jnp.maximum(top, placed(lax.optimization_barrier(jnp.max(scores, axis=2)), level_k, phase, jnp.float32(-jnp.inf)))
    total = jnp.zeros((TOKENS,), jnp.float32)
    expo_list = []
    for level_k in range(LEVELS):
        phase = phases[level_k]
        expo = jnp.exp(score_list[level_k] - taken(top, level_k, phase)[:, :, None])
        expo_list.append(expo)
        total = total + placed(lax.optimization_barrier(jnp.sum(expo, axis=2)), level_k, phase, jnp.float32(0.0))
    weight_list, low_list = ([], [])
    attended_sum = jnp.zeros((TOKENS, HD), jnp.float32)
    for level_k in range(LEVELS):
        phase = phases[level_k]
        weights = expo_list[level_k] / taken(total, level_k, phase)[:, :, None]
        weight_low = lowered(weights).astype(jnp.float32)
        weight_list.append(weights)
        low_list.append(weight_low)
        attended_sum = attended_sum + placed(batched('nqk,nkd->nqd', weight_low, value_list[level_k]), level_k, phase, jnp.float32(0.0))
    attended_low = lowered(attended_sum)
    attended_wide = attended_low.astype(jnp.float32)
    forward_part = jnp.dot(attended_low, w_output, preferred_element_type=jnp.float32)
    upstream = lowered(jnp.dot(cotangent, w_output.T, preferred_element_type=jnp.float32))
    upstream_wide = upstream.astype(jnp.float32)
    delta = lax.optimization_barrier(jnp.sum(upstream_wide * attended_wide, axis=1))
    grad_query = jnp.zeros((TOKENS, HD), jnp.float32)
    grad_key = jnp.zeros((TOKENS, HD), jnp.float32)
    grad_value = jnp.zeros((TOKENS, HD), jnp.float32)
    for level_k in range(LEVELS):
        phase = phases[level_k]
        upstream_taken = taken(upstream_wide, level_k, phase)
        delta_taken = taken(delta, level_k, phase)
        dots = batched('nqd,nkd->nqk', upstream_taken, value_list[level_k])
        slopes = lowered(weight_list[level_k] * (dots - delta_taken[:, :, None])).astype(jnp.float32)
        grad_query = grad_query + placed(batched('nqk,nkd->nqd', slopes, key_list[level_k]), level_k, phase, jnp.float32(0.0))
        grad_key = grad_key + placed(batched('nqk,nqd->nkd', slopes, query_list[level_k]), level_k, phase, jnp.float32(0.0))
        grad_value = grad_value + placed(batched('nqk,nqd->nkd', low_list[level_k], upstream_taken), level_k, phase, jnp.float32(0.0))
    grad_query = lowered(grad_query * scaling)
    grad_key = lowered(grad_key)
    grad_value = lowered(grad_value)
    back = jnp.dot(grad_query, w_query.T, preferred_element_type=jnp.float32)
    back = back + jnp.dot(grad_key, w_key.T, preferred_element_type=jnp.float32)
    back = back + jnp.dot(grad_value, w_value.T, preferred_element_type=jnp.float32)
    return (forward_part, back)

def reference(tokens, w_qkv, w_out, offsets, cotangent):

    def group_step(carry, group):
        out_sum, in_sum = carry
        out_part = jnp.zeros((TOKENS, D), jnp.float32)
        in_part = jnp.zeros((TOKENS, D), jnp.float32)
        for local in range(HEADS_DEV):
            head = (group * HEADS_DEV + local).astype(jnp.int32)
            start = (head * HD).astype(jnp.int32)
            w_query = lax.dynamic_slice_in_dim(w_qkv[0], start, HD, 1)
            w_key = lax.dynamic_slice_in_dim(w_qkv[1], start, HD, 1)
            w_value = lax.dynamic_slice_in_dim(w_qkv[2], start, HD, 1)
            w_output = lax.dynamic_slice_in_dim(w_out, start, HD, 0)
            phase_all = lax.dynamic_index_in_dim(offsets, head, keepdims=False)
            forward_part, back = one_head(tokens, cotangent, w_query, w_key, w_value, w_output, phase_all)
            out_part = out_part + forward_part
            in_part = in_part + back
        out_sum = out_sum + lowered(out_part).astype(jnp.float32)
        in_sum = in_sum + lowered(in_part).astype(jnp.float32)
        return ((out_sum, in_sum), group)
    zeros = jnp.zeros((TOKENS, D), jnp.float32)
    (out_sum, in_sum), unused = lax.scan(group_step, (zeros, zeros), jnp.arange(N_HEAD, dtype=jnp.int32))
    return (out_sum.astype(jnp.bfloat16), in_sum.astype(jnp.bfloat16))
```

```python
import math

import jax
import jax.numpy as jnp
from jax import lax
from jax.experimental import pallas as pl
from jax.experimental.pallas import tpu as pltpu
from jax.sharding import PartitionSpec as P

MESH = pl.DeviceIdType.MESH
F32, BF16 = jnp.float32, jnp.bfloat16
ROWS = 512
MODEL = 2048
HD = 128
HEADS = 2
RING = 8
ALL = 1280
PAIR, QUAD0, QUAD1, OCT0, OCT1, OCT2, OCT3 = 512, 768, 896, 1024, 1088, 1152, 1216
COLS = 256
NEG = float("-inf")


def nn(a, b):
    return jnp.dot(a, b, preferred_element_type=F32)


def nt(a, b):
    return lax.dot_general(a, b, (((1,), (1,)), ((), ())), preferred_element_type=F32)


def tn(a, b):
    return lax.dot_general(a, b, (((0,), (0,)), ((), ())), preferred_element_type=F32)


def slot_table():
    tables = []
    for k in range(1, RING):
        code = 0
        for d in range(RING):
            source = (d - k) % RING
            inner = d % 4 in (1, 2)
            side = 1 if d % 2 == 1 else -1
            out_dist = (source - d) * side % RING
            in_dist = (d - source) * side % RING
            if source // 2 == d // 2:
                slot = 0
            elif source // 4 == d // 4:
                slot = 1 if source % 4 in (1, 2) else 2
            elif inner:
                slot = {2: 3, 3: 4}[in_dist] if in_dist in (2, 3) else {3: 5, 4: 6}[out_dist]
            else:
                slot = 2 + out_dist
            code += slot * 8**d
        tables.append(code)
    return tables


SLOTS = slot_table()


def kernel(
    tok_hbm, wqkv_hbm, wo_hbm, off_ref, cot_hbm, out_ref, ing_ref,
    tok, wqkv, wo, cot, raw, kv, qd, perm, unperm, mask_a, mask_b, mask_p, mask_q,
    grads, att_p, gcat, att, gall, stat, stat_g,
    own, sib_out, sib_in, far, half_in, near, near_in,
    load_sem, kv_send, kv_recv, qd_send, qd_recv, st_send, st_recv, rs_send, rs_recv,
):
    seq = lax.axis_index("seq")
    head = lax.axis_index("head")
    z = lax.rem(seq, RING)
    base = seq - z
    odd = lax.rem(z, 2)
    partner = (base + z + 1 - 2 * odd, head)
    outer = (base + lax.rem(z + 2 * odd + RING - 1, RING), head)
    inner = lax.rem((lax.rem(z, 4) + 1) // 2, 2) == 1
    edge = jnp.logical_not(inner)
    x, core = head // 2, lax.rem(head, 2)
    sibling = (seq, head + 1 - 2 * core)
    right = (seq, lax.rem(x + 1, 4) * 2 + core)
    left = (seq, lax.rem(x + 3, 4) * 2 + core)

    loads = [
        pltpu.make_async_copy(tok_hbm, tok, load_sem.at[0]),
        pltpu.make_async_copy(wqkv_hbm.at[1], wqkv.at[1], load_sem.at[1]),
        pltpu.make_async_copy(wqkv_hbm.at[2], wqkv.at[2], load_sem.at[2]),
        pltpu.make_async_copy(wqkv_hbm.at[0], wqkv.at[0], load_sem.at[3]),
        pltpu.make_async_copy(cot_hbm, cot, load_sem.at[4]),
        pltpu.make_async_copy(wo_hbm, wo, load_sem.at[5]),
    ]
    for copy in loads:
        copy.start()

    barrier = pltpu.get_barrier_semaphore()
    peers = [(base + lax.rem(z + k, RING), head) for k in range(1, RING)]
    for device in peers + [sibling, right, left]:
        pl.semaphore_signal(barrier, inc=1, device_id=device, device_id_type=MESH)

    index = lax.broadcasted_iota(jnp.int32, (ROWS, 128), 0)
    lane = lax.broadcasted_iota(jnp.int32, (ROWS, 128), 1)
    for h in range(HEADS):
        offset = off_ref[h]
        block = index >> 6
        turned = ((block & 1) << 2) | (block & 2) | (block >> 2)
        old = ((index & 63) << 3) + ((turned + offset) & 7)
        rest = ((index & 7) - offset) & 7
        new = ((((rest & 1) << 2) | (rest & 2) | (rest >> 2)) << 6) + (index >> 3)
        for c in range(ROWS // 128):
            perm[h, :, c * 128 : (c + 1) * 128] = jnp.where(old == lane + c * 128, 1.0, 0.0).astype(BF16)
            unperm[h, :, c * 128 : (c + 1) * 128] = jnp.where(new == lane + c * 128, 1.0, 0.0).astype(BF16)

    def levels(key, query, start):
        far_end = jnp.maximum(key, query)
        count = jnp.full(key.shape, float(start), F32)
        for limit in (256, 128, 64):
            count = count + jnp.where(far_end < limit, 1.0, 0.0)
        return count

    mask_a[0:512] = levels(index, lane, 1)
    mask_a[512:768] = levels(index[0:256], lane[0:256], 0)
    quad_mask = levels(index[0:128], lane[0:128], -1)
    mask_a[768:896] = quad_mask
    mask_a[896:1024] = quad_mask
    mask_a[1024:1280] = jnp.where(lane[0:256] < 64, 1.0, 0.0)
    mask_b[0:512] = levels(index, lane + 128, 1)
    mask_b[512:768] = levels(index[0:256], lane[0:256] + 128, 0)
    mask_p[:, 0:128] = levels(index[0:256], lane[0:256], 0)
    mask_p[:, 128:256] = levels(index[0:256], lane[0:256] + 128, 0)
    mask_q[:, 0:128] = quad_mask
    mask_q[:, 128:256] = quad_mask

    def project(left_part, right_part):
        for h in range(HEADS):
            raw[:, h * 256 : h * 256 + 128] = left_part[:, h * 128 : (h + 1) * 128]
            raw[:, h * 256 + 128 : h * 256 + 256] = right_part[:, h * 128 : (h + 1) * 128]

    def permute(into):
        for h in range(HEADS):
            into[0:ROWS, h * 256 : (h + 1) * 256] = nn(perm[h], raw[:, h * 256 : (h + 1) * 256]).astype(BF16)

    def remote(src, dst, send, recv, device):
        return pltpu.make_async_remote_copy(
            src_ref=src, dst_ref=dst, send_sem=send, recv_sem=recv, device_id=device, device_id_type=MESH
        )

    steps = {
        "p1": ((0, 256, PAIR), (0, 256, PAIR), partner),
        "o1": ((0, 128, QUAD0), (0, 64, OCT0), outer),
        "o2": ((PAIR, 128, QUAD1), (PAIR, 64, OCT1), outer),
        "p2": ((QUAD0, 128, QUAD0), (OCT0, 64, OCT0), partner),
        "o3": ((OCT0, 64, OCT2), (QUAD0, 64, OCT2), outer),
        "p3": ((QUAD1, 128, QUAD1), (OCT1, 64, OCT1), partner),
        "o4": ((OCT1, 64, OCT3), (QUAD1, 64, OCT3), outer),
    }
    arrivals = {
        "p1": ((PAIR, 256), (PAIR, 256)),
        "o1": ((QUAD0, 128), (OCT0, 64)),
        "o2": ((QUAD1, 128), (OCT1, 64)),
        "p2": ((OCT0, 64), (QUAD0, 128)),
        "o3": ((OCT2, 64), (OCT2, 64)),
        "p3": ((OCT1, 64), (QUAD1, 128)),
        "o4": ((OCT3, 64), (OCT3, 64)),
    }
    order = {name: i for i, name in enumerate(steps)}

    class Gather:
        def __init__(self, buf, send, recv):
            self.buf, self.send_sem, self.recv_sem = buf, send, recv

        def each(self, name, act):
            in_case, edge_case, device = steps[name]
            if in_case == edge_case:
                act(in_case, device)
            else:
                pl.when(inner)(lambda: act(in_case, device))
                pl.when(edge)(lambda: act(edge_case, device))

        def copy(self, name, case, device):
            src, rows, dst = case
            i = order[name]
            return remote(
                self.buf.at[pl.ds(src, rows)], self.buf.at[pl.ds(dst, rows)],
                self.send_sem.at[i], self.recv_sem.at[i], device,
            )

        def send(self, name):
            self.each(name, lambda case, device: self.copy(name, case, device).start())

        def sent(self, name):
            self.each(name, lambda case, device: self.copy(name, case, device).wait_send())

        def arrive(self, name):
            i, device = order[name], steps[name][2]

            def act(case):
                spot = self.buf.at[pl.ds(case[0], case[1])]
                remote(spot, spot, self.send_sem.at[i], self.recv_sem.at[i], device).wait_recv()

            in_case, edge_case = arrivals[name]
            if in_case == edge_case:
                act(in_case)
            else:
                pl.when(inner)(lambda: act(in_case))
                pl.when(edge)(lambda: act(edge_case))

    kv_ring = Gather(kv, kv_send, kv_recv)
    qd_ring = Gather(qd, qd_send, qd_recv)

    loads[0].wait()
    loads[1].wait()
    keys = nn(tok[...], wqkv[1]).astype(BF16)
    loads[2].wait()
    values = nn(tok[...], wqkv[2]).astype(BF16)
    project(keys, values)
    permute(kv)

    pl.semaphore_wait(barrier, len(peers) + 3)
    kv_ring.send("p1")
    kv_ring.send("o1")

    loads[3].wait()
    queries = (nn(tok[...], wqkv[0]) * (1.0 / math.sqrt(HD))).astype(BF16)
    loads[4].wait()
    loads[5].wait()
    upstream = nt(cot[...], wo[...]).astype(BF16)
    project(queries, upstream)
    permute(qd)

    def block(h, first, width, depth, mask, fresh):
        k, v = slice(h * 256, h * 256 + 128), slice(h * 256 + 128, h * 256 + 256)
        q_rows, d_rows = qd[first : first + width, k], qd[first : first + width, v]
        s = nt(kv[0:depth, k], q_rows)
        if mask is not None:
            s = jnp.where(mask[...] > 0.0, s, NEG)
        top = jnp.max(s, axis=0, keepdims=True)
        e = jnp.exp(s - top)
        if mask is not None:
            e = e * mask[...]
        inv = 1.0 / jnp.sum(e, axis=0, keepdims=True)
        p = e * inv
        p_low = p.astype(BF16)
        attended = tn(p_low, kv[0:depth, v]).astype(BF16)
        att_p[first : first + width, h * 128 : (h + 1) * 128] = attended
        product = d_rows.astype(F32) * attended.astype(F32)
        delta = jnp.sum(product.T, axis=0, keepdims=True)
        stat[h : h + 1, first : first + width] = top
        stat[2 + h : 3 + h, first : first + width] = inv
        stat[4 + h : 5 + h, first : first + width] = delta
        slope = (p * (nt(kv[0:depth, v], d_rows) - delta)).astype(BF16)
        gcat[first : first + width, h * 384 : h * 384 + 128] = (
            tn(slope, kv[0:depth, k]) * (1.0 / math.sqrt(HD))
        ).astype(BF16)
        dk = nn(slope[0:ROWS], q_rows)
        dv = nn(p_low[0:ROWS], d_rows)
        if fresh:
            grads[h, :, 0:128] = dk
            grads[h, :, 128:256] = dv
        else:
            grads[h, :, 0:128] += dk
            grads[h, :, 128:256] += dv

    block(0, 256, 256, ROWS, None, True)
    kv_ring.arrive("o1")
    kv_ring.send("p2")
    block(1, 256, 256, ROWS, None, True)
    kv_ring.arrive("p1")
    kv_ring.send("o2")
    qd_ring.send("p1")
    qd_ring.send("o1")
    for h in range(HEADS):
        block(h, 128, 128, 768, mask_b, False)
    kv_ring.arrive("o2")
    kv_ring.send("p3")
    kv_ring.arrive("p2")
    kv_ring.send("o3")
    kv_ring.arrive("p3")
    kv_ring.send("o4")
    qd_ring.arrive("o1")
    qd_ring.send("p2")
    kv_ring.arrive("o3")
    kv_ring.arrive("o4")
    qd_ring.arrive("p1")
    qd_ring.send("o2")
    for h in range(HEADS):
        block(h, 0, 128, ALL, mask_a, False)

    st_copies = []
    for k in range(1, RING):
        spot = lax.rem(z + k, RING)
        slot = SLOTS[k - 1]
        power = 1
        digit = 0
        for d in range(RING):
            here = 1 - (spot - d) * (spot - d)
            here = (here + jnp.abs(here)) // 2
            digit = digit + here * (slot // 8**d % 8)
        copy = remote(
            stat.at[:, pl.ds(0, 256)], stat_g.at[digit], st_send.at[k - 1], st_recv.at[k - 1], peers[k - 1]
        )
        copy.start()
        st_copies.append(copy)

    qd_ring.arrive("o2")
    qd_ring.send("p3")
    qd_ring.arrive("p2")
    qd_ring.send("o3")

    class Scatter:
        def __init__(self, r):
            self.r = r
            self.copies = []

        def sems(self, i):
            return rs_send.at[self.r, i], rs_recv.at[self.r, i]

        def send(self, i, src, dst, device):
            copy = remote(src, dst, *self.sems(i), device)
            copy.start()
            self.copies.append(copy)

        def arrive(self, i, dst, device):
            remote(dst, dst, *self.sems(i), device).wait_recv()

        def compute(self, product):
            r = self.r
            for dx in (2, 1, 3, 0):
                target = lax.rem(x + dx, 4) * 2
                sib_out[r, dx] = product(target + 1 - core).astype(BF16)
                self.send(dx, sib_out.at[r, dx], sib_in.at[r, dx], sibling)
                own[r, dx] = product(target + core)

        def pair_sum(self, dx):
            r = self.r
            self.arrive(dx, sib_in.at[r, dx], sibling)
            return own[r, dx] + sib_in[r, dx].astype(F32)

        def first(self):
            r = self.r
            far[r] = self.pair_sum(2).astype(BF16)
            self.send(4, far.at[r, pl.ds(0, 256)], half_in.at[r, 0], right)
            self.send(5, far.at[r, pl.ds(256, 256)], half_in.at[r, 1], left)
            own[r, 1] = self.pair_sum(1)
            near[r, 0, 256:512] = own[r, 1, 256:512].astype(BF16)
            self.send(6, near.at[r, 0, pl.ds(256, 256)], near_in.at[r, 0, pl.ds(256, 256)], right)
            own[r, 3] = self.pair_sum(3)
            near[r, 1, 0:256] = own[r, 3, 0:256].astype(BF16)
            self.send(7, near.at[r, 1, pl.ds(0, 256)], near_in.at[r, 1, pl.ds(0, 256)], left)
            own[r, 0] = self.pair_sum(0)

        def second(self):
            r = self.r
            self.arrive(4, half_in.at[r, 0], right)
            near[r, 0, 0:256] = (own[r, 1, 0:256] + half_in[r, 0].astype(F32)).astype(BF16)
            self.send(8, near.at[r, 0, pl.ds(0, 256)], near_in.at[r, 0, pl.ds(0, 256)], right)
            self.arrive(5, half_in.at[r, 1], left)
            near[r, 1, 256:512] = (own[r, 3, 256:512] + half_in[r, 1].astype(F32)).astype(BF16)
            self.send(9, near.at[r, 1, pl.ds(256, 256)], near_in.at[r, 1, pl.ds(256, 256)], left)

        def last(self, into):
            r = self.r
            self.arrive(6, near_in.at[r, 0, pl.ds(256, 256)], right)
            self.arrive(7, near_in.at[r, 1, pl.ds(0, 256)], left)
            self.arrive(8, near_in.at[r, 0, pl.ds(0, 256)], right)
            self.arrive(9, near_in.at[r, 1, pl.ds(256, 256)], left)
            into[...] = (own[r, 0] + near_in[r, 0].astype(F32) + near_in[r, 1].astype(F32)).astype(BF16)

        def drain(self):
            for copy in self.copies:
                copy.wait_send()

    for h in range(HEADS):
        att[:, h * 128 : (h + 1) * 128] = nn(unperm[h], att_p[:, h * 128 : (h + 1) * 128]).astype(BF16)
    scatter_out = Scatter(0)
    scatter_out.compute(
        lambda target: nn(att[...], wo[:, pl.ds(pl.multiple_of(target * COLS, COLS), COLS)])
    )
    qd_ring.arrive("p3")
    qd_ring.send("o4")
    scatter_out.first()

    for k in range(1, RING):
        remote(
            stat_g.at[0], stat_g.at[0], st_send.at[k - 1], st_recv.at[k - 1], peers[k - 1]
        ).wait_recv()

    def far_block(h, first, depth, stats, mask):
        k, v = slice(h * 256, h * 256 + 128), slice(h * 256 + 128, h * 256 + 256)
        q_rows, d_rows = qd[first : first + 256, k], qd[first : first + 256, v]
        top, inv, delta = (stats[i : i + 1] for i in (h, 2 + h, 4 + h))
        p = jnp.exp(nt(kv[0:depth, k], q_rows) - top) * inv
        if mask is not None:
            p = p * mask[...]
        p_low = p.astype(BF16)
        slope = (p * (nt(kv[0:depth, v], d_rows) - delta)).astype(BF16)
        grads[h, 0:depth, 0:128] += nn(slope, q_rows)
        grads[h, 0:depth, 128:256] += nn(p_low, d_rows)

    for h in range(HEADS):
        far_block(h, PAIR, 256, stat_g[0], mask_p)
    quad_stat = jnp.concatenate([stat_g[1, :, 0:128], stat_g[2, :, 0:128]], 1)
    for h in range(HEADS):
        far_block(h, QUAD0, 128, quad_stat, mask_q)
    scatter_out.second()
    qd_ring.arrive("o3")
    qd_ring.arrive("o4")
    low_lanes = lax.broadcasted_iota(jnp.int32, (8, 128), 1) < 64
    oct_stat = jnp.concatenate(
        [
            jnp.where(low_lanes, stat_g[a, :, 0:128], pltpu.roll(stat_g[a + 1, :, 0:128], 64, 1))
            for a in (3, 5)
        ],
        1,
    )
    for h in range(HEADS):
        far_block(h, OCT0, 64, oct_stat, None)

    for h in range(HEADS):
        gcat[:, h * 384 + 128 : h * 384 + 384] = grads[h].astype(BF16)
        turned = nn(unperm[h], gcat[:, h * 384 : (h + 1) * 384]).astype(BF16)
        for part in range(3):
            gall[part, :, h * 128 : (h + 1) * 128] = turned[:, part * 128 : (part + 1) * 128]

    def back(target):
        rows = pl.ds(pl.multiple_of(target * COLS, COLS), COLS)
        return nt(gall[0], wqkv[0, rows]) + nt(gall[1], wqkv[1, rows]) + nt(gall[2], wqkv[2, rows])

    scatter_in = Scatter(1)
    scatter_in.compute(back)
    scatter_in.first()
    scatter_out.last(out_ref)
    scatter_in.second()
    scatter_in.last(ing_ref)

    for name in steps:
        kv_ring.sent(name)
        qd_ring.sent(name)
    for copy in st_copies:
        copy.wait_send()
    scatter_out.drain()
    scatter_in.drain()


def on_device(tokens, w_qkv, w_out, offsets, cotangent):
    whole = pl.BlockSpec(memory_space=pl.ANY)
    vmem = pl.BlockSpec(memory_space=pltpu.VMEM)
    return pl.pallas_call(
        kernel,
        out_shape=(jax.ShapeDtypeStruct((ROWS, COLS), BF16),) * 2,
        in_specs=[whole, whole, whole, pl.BlockSpec(memory_space=pltpu.SMEM), whole],
        out_specs=(vmem, vmem),
        scratch_shapes=[
            pltpu.VMEM((ROWS, MODEL), BF16),
            pltpu.VMEM((3, MODEL, COLS), BF16),
            pltpu.VMEM((COLS, MODEL), BF16),
            pltpu.VMEM((ROWS, MODEL), BF16),
            pltpu.VMEM((ROWS, 512), BF16),
            pltpu.VMEM((ALL, 512), BF16),
            pltpu.VMEM((ALL, 512), BF16),
            pltpu.VMEM((HEADS, ROWS, ROWS), BF16),
            pltpu.VMEM((HEADS, ROWS, ROWS), BF16),
            pltpu.VMEM((ALL, 128), F32),
            pltpu.VMEM((768, 128), F32),
            pltpu.VMEM((256, 256), F32),
            pltpu.VMEM((128, 256), F32),
            pltpu.VMEM((HEADS, ROWS, 256), F32),
            pltpu.VMEM((ROWS, 256), BF16),
            pltpu.VMEM((ROWS, 768), BF16),
            pltpu.VMEM((ROWS, 256), BF16),
            pltpu.VMEM((3, ROWS, 256), BF16),
            pltpu.VMEM((8, ROWS), F32),
            pltpu.VMEM((7, 8, 256), F32),
            pltpu.VMEM((2, 4, ROWS, COLS), F32),
            pltpu.VMEM((2, 4, ROWS, COLS), BF16),
            pltpu.VMEM((2, 4, ROWS, COLS), BF16),
            pltpu.VMEM((2, ROWS, COLS), BF16),
            pltpu.VMEM((2, 2, 256, COLS), BF16),
            pltpu.VMEM((2, 2, ROWS, COLS), BF16),
            pltpu.VMEM((2, 2, ROWS, COLS), BF16),
            pltpu.SemaphoreType.DMA((6,)),
            pltpu.SemaphoreType.DMA((7,)),
            pltpu.SemaphoreType.DMA((7,)),
            pltpu.SemaphoreType.DMA((7,)),
            pltpu.SemaphoreType.DMA((7,)),
            pltpu.SemaphoreType.DMA((7,)),
            pltpu.SemaphoreType.DMA((7,)),
            pltpu.SemaphoreType.DMA((2, 10)),
            pltpu.SemaphoreType.DMA((2, 10)),
        ],
        compiler_params=pltpu.CompilerParams(
            collective_id=0, has_side_effects=True, vmem_limit_bytes=52 * 1024 * 1024
        ),
    )(tokens, w_qkv, w_out, offsets, cotangent)


def solution(mesh):
    in_specs = (P("seq", None), P(None, None, "head"), P("head", None), P("head"), P("seq", None))
    out_specs = (P("seq", "head"), P("seq", "head"))
    return jax.shard_map(on_device, mesh=mesh, in_specs=in_specs, out_specs=out_specs, check_vma=False)
```

```python
import math

import jax
import jax.numpy as jnp
from jax import lax
from jax.experimental import pallas as pl
from jax.experimental.pallas import tpu as pltpu
from jax.sharding import PartitionSpec as P

MESH = pl.DeviceIdType.MESH
F32, BF16 = jnp.float32, jnp.bfloat16
ROWS = 512
MODEL = 2048
HD = 128
HEADS = 2
RING = 8
ALL = 1280
PAIR, QUAD0, QUAD1, OCT0, OCT1, OCT2, OCT3 = 512, 768, 896, 1024, 1088, 1152, 1216
COLS = 256
NEG = float("-inf")


def nn(a, b):
    return jnp.dot(a, b, preferred_element_type=F32)


def nt(a, b):
    return lax.dot_general(a, b, (((1,), (1,)), ((), ())), preferred_element_type=F32)


def tn(a, b):
    return lax.dot_general(a, b, (((0,), (0,)), ((), ())), preferred_element_type=F32)


def slot_table():
    tables = []
    for k in range(1, RING):
        code = 0
        for d in range(RING):
            source = (d - k) % RING
            inner = d % 4 in (1, 2)
            side = 1 if d % 2 == 1 else -1
            out_dist = (source - d) * side % RING
            in_dist = (d - source) * side % RING
            if source // 2 == d // 2:
                slot = 0
            elif source // 4 == d // 4:
                slot = 1 if source % 4 in (1, 2) else 2
            elif inner:
                slot = {2: 3, 3: 4}[in_dist] if in_dist in (2, 3) else {3: 5, 4: 6}[out_dist]
            else:
                slot = 2 + out_dist
            code += slot * 8**d
        tables.append(code)
    return tables


SLOTS = slot_table()


def kernel(
    tok_hbm, wqkv_hbm, wo_hbm, off_hbm, cot_hbm, out_ref, ing_ref,
    tok, wkv, wq, wo, cot, off_ref, raw, kv, qd, perm, unperm, mask_a, mask_b, mask_p, mask_q,
    grads, att_p, dq_p, gkv_p, att, gq, gkv, acc, stat, stat_g,
    own, sib_out, sib_in, far, half_in, near, near_in,
    load_sem, ring_send, ring_recv, st_send, st_recv, rs_send, rs_recv,
):
    seq = lax.axis_index("seq")
    head = lax.axis_index("head")
    z = lax.rem(seq, RING)
    base = seq - z
    odd = lax.rem(z, 2)
    partner = (base + z + 1 - 2 * odd, head)
    outer = (base + lax.rem(z + 2 * odd + RING - 1, RING), head)
    inner = lax.rem((lax.rem(z, 4) + 1) // 2, 2) == 1
    edge = jnp.logical_not(inner)
    x, core = head // 2, lax.rem(head, 2)
    sibling = (seq, head + 1 - 2 * core)
    right = (seq, lax.rem(x + 1, 4) * 2 + core)
    left = (seq, lax.rem(x + 3, 4) * 2 + core)

    loads = [
        pltpu.make_async_copy(off_hbm, off_ref, load_sem.at[0]),
        pltpu.make_async_copy(tok_hbm, tok, load_sem.at[1]),
    ]
    for h in range(HEADS):
        for part in range(2):
            loads.append(
                pltpu.make_async_copy(
                    wqkv_hbm.at[1 + part, :, pl.ds(h * 128, 128)],
                    wkv.at[:, pl.ds(h * 256 + part * 128, 128)],
                    load_sem.at[2 + 2 * h + part],
                )
            )
    late_loads = [
        pltpu.make_async_copy(wqkv_hbm.at[0], wq, load_sem.at[6]),
        pltpu.make_async_copy(cot_hbm, cot, load_sem.at[7]),
        pltpu.make_async_copy(wo_hbm, wo, load_sem.at[8]),
    ]
    for copy in loads:
        copy.start()

    barrier = pltpu.get_barrier_semaphore()
    peers = [(base + lax.rem(z + k, RING), head) for k in range(1, RING)]
    for device in peers + [sibling, right, left]:
        pl.semaphore_signal(barrier, inc=1, device_id=device, device_id_type=MESH)

    index = lax.broadcasted_iota(jnp.int32, (ROWS, 128), 0)
    lane = lax.broadcasted_iota(jnp.int32, (ROWS, 128), 1)

    def levels(key, query, start):
        far_end = jnp.maximum(key, query)
        count = jnp.full(key.shape, float(start), F32)
        for limit in (256, 128, 64):
            count = count + jnp.where(far_end < limit, 1.0, 0.0)
        return count

    mask_a[0:512] = levels(index, lane, 1)
    mask_a[512:768] = levels(index[0:256], lane[0:256], 0)
    quad_mask = levels(index[0:128], lane[0:128], -1)
    mask_a[768:896] = quad_mask
    mask_a[896:1024] = quad_mask
    mask_a[1024:1280] = jnp.where(lane[0:256] < 64, 1.0, 0.0)
    mask_b[0:512] = levels(index, lane + 128, 1)
    mask_b[512:768] = levels(index[0:256], lane[0:256] + 128, 0)
    mask_p[:, 0:128] = levels(index[0:256], lane[0:256], 0)
    mask_p[:, 128:256] = levels(index[0:256], lane[0:256] + 128, 0)
    mask_q[:, 0:128] = quad_mask
    mask_q[:, 128:256] = quad_mask
    for copy in late_loads:
        copy.start()

    loads[0].wait()
    for h in range(HEADS):
        offset = off_ref[h]
        block = index >> 6
        turned = ((block & 1) << 2) | (block & 2) | (block >> 2)
        old = ((index & 63) << 3) + ((turned + offset) & 7)
        rest = ((index & 7) - offset) & 7
        new = ((((rest & 1) << 2) | (rest & 2) | (rest >> 2)) << 6) + (index >> 3)
        for c in range(ROWS // 128):
            perm[h, :, c * 128 : (c + 1) * 128] = jnp.where(old == lane + c * 128, 1.0, 0.0).astype(BF16)
            unperm[h, :, c * 128 : (c + 1) * 128] = jnp.where(new == lane + c * 128, 1.0, 0.0).astype(BF16)

    def remote(src, dst, send, recv, device):
        return pltpu.make_async_remote_copy(
            src_ref=src, dst_ref=dst, send_sem=send, recv_sem=recv, device_id=device, device_id_type=MESH
        )

    steps = {
        "p1": ((0, 128, PAIR), (0, 128, PAIR), partner),
        "p1b": ((128, 128, PAIR + 128), (128, 128, PAIR + 128), partner),
        "o1": ((0, 128, QUAD0), (0, 64, OCT0), outer),
        "o2": ((PAIR, 128, QUAD1), (PAIR, 64, OCT1), outer),
        "p2": ((QUAD0, 128, QUAD0), (OCT0, 64, OCT0), partner),
        "o3": ((OCT0, 64, OCT2), (QUAD0, 64, OCT2), outer),
        "p3": ((QUAD1, 128, QUAD1), (OCT1, 64, OCT1), partner),
        "o4": ((OCT1, 64, OCT3), (QUAD1, 64, OCT3), outer),
    }
    arrivals = {
        "p1": ((PAIR, 128), (PAIR, 128)),
        "p1b": ((PAIR + 128, 128), (PAIR + 128, 128)),
        "o1": ((QUAD0, 128), (OCT0, 64)),
        "o2": ((QUAD1, 128), (OCT1, 64)),
        "p2": ((OCT0, 64), (QUAD0, 128)),
        "o3": ((OCT2, 64), (OCT2, 64)),
        "p3": ((OCT1, 64), (QUAD1, 128)),
        "o4": ((OCT3, 64), (OCT3, 64)),
    }
    order = {name: i for i, name in enumerate(steps)}
    onward = {"o1": "p2", "p1": "o2", "o2": "p3", "p2": "o3", "p3": "o4"}

    class Gather:
        def __init__(self, buf, send, recv):
            self.buf, self.send_sem, self.recv_sem = buf, send, recv

        def each(self, name, act):
            in_case, edge_case, device = steps[name]
            if in_case == edge_case:
                act(in_case, device)
            else:
                pl.when(inner)(lambda: act(in_case, device))
                pl.when(edge)(lambda: act(edge_case, device))

        def copy(self, name, case, device):
            src, rows, dst = case
            i = order[name]
            return remote(
                self.buf.at[pl.ds(src, rows)], self.buf.at[pl.ds(dst, rows)],
                self.send_sem.at[i], self.recv_sem.at[i], device,
            )

        def send(self, name):
            self.each(name, lambda case, device: self.copy(name, case, device).start())

        def sent(self, name):
            self.each(name, lambda case, device: self.copy(name, case, device).wait_send())

        def arrive(self, name):
            i, device = order[name], steps[name][2]

            def act(case):
                spot = self.buf.at[pl.ds(case[0], case[1])]
                remote(spot, spot, self.send_sem.at[i], self.recv_sem.at[i], device).wait_recv()

            in_case, edge_case = arrivals[name]
            if in_case == edge_case:
                act(in_case)
            else:
                pl.when(inner)(lambda: act(in_case))
                pl.when(edge)(lambda: act(edge_case))

        def own(self):
            self.send("o1")
            self.send("p1")

        def on(self, name):
            self.arrive(name)
            self.send(onward[name])

    rings = [Gather(buf.at[h], ring_send.at[i, h], ring_recv.at[i, h]) for i, buf in enumerate((kv, qd)) for h in range(HEADS)]
    kv0, kv1, qd0, qd1 = rings

    for copy in loads[1:]:
        copy.wait()
    raw[...] = nn(tok[...], wkv[...]).astype(BF16)
    kv[0, 0:ROWS] = nn(perm[0], raw[:, 0:256]).astype(BF16)
    pl.semaphore_wait(barrier, len(peers) + 3)
    kv0.own()
    kv[1, 0:ROWS] = nn(perm[1], raw[:, 256:512]).astype(BF16)
    late_loads[0].wait()
    queries = (nn(tok[...], wq[...]) * (1.0 / math.sqrt(HD))).astype(BF16)
    kv1.own()
    late_loads[1].wait()
    late_loads[2].wait()
    upstream = nt(cot[...], wo[...]).astype(BF16)
    for h in range(HEADS):
        raw[:, h * 256 : h * 256 + 128] = queries[:, h * 128 : (h + 1) * 128]
        raw[:, h * 256 + 128 : h * 256 + 256] = upstream[:, h * 128 : (h + 1) * 128]
    kv0.on("o1")
    kv0.on("p1")
    kv0.send("p1b")
    for h in range(HEADS):
        qd[h, 0:ROWS] = nn(perm[h], raw[:, h * 256 : (h + 1) * 256]).astype(BF16)

    first, second = slice(0, 128), slice(128, 256)

    def block(h, start, width, depth, mask, fresh):
        q_rows, d_rows = qd[h, start : start + width, first], qd[h, start : start + width, second]
        s = nt(kv[h, 0:depth, first], q_rows)
        if mask is not None:
            s = jnp.where(mask[...] > 0.0, s, NEG)
        top = jnp.max(s, axis=0, keepdims=True)
        e = jnp.exp(s - top)
        if mask is not None:
            e = e * mask[...]
        inv = 1.0 / jnp.sum(e, axis=0, keepdims=True)
        p = e * inv
        p_low = p.astype(BF16)
        attended = tn(p_low, kv[h, 0:depth, second]).astype(BF16)
        att_p[h, start : start + width] = attended
        product = d_rows.astype(F32) * attended.astype(F32)
        delta = jnp.sum(product.T, axis=0, keepdims=True)
        stat[h : h + 1, start : start + width] = top
        stat[2 + h : 3 + h, start : start + width] = inv
        stat[4 + h : 5 + h, start : start + width] = delta
        slope = (p * (nt(kv[h, 0:depth, second], d_rows) - delta)).astype(BF16)
        dq_p[h, start : start + width] = (tn(slope, kv[h, 0:depth, first]) * (1.0 / math.sqrt(HD))).astype(BF16)
        dk = nn(slope[0:ROWS], q_rows)
        dv = nn(p_low[0:ROWS], d_rows)
        if fresh:
            grads[h, :, first] = dk
            grads[h, :, second] = dv
        else:
            grads[h, :, first] += dk
            grads[h, :, second] += dv

    block(0, 256, 256, ROWS, None, True)
    kv1.on("o1")
    kv1.on("p1")
    block(1, 256, 256, ROWS, None, True)
    kv0.on("o2")
    kv0.on("p2")
    kv0.arrive("p1b")
    block(0, 128, 128, 768, mask_b, False)
    kv1.on("o2")
    kv1.send("p1b")
    kv1.on("p2")
    qd0.own()
    qd1.own()
    kv0.on("p3")
    kv1.on("p3")
    qd0.on("o1")

    def inner_passes():
        qd0.on("p1")
        qd1.on("o1")

    pl.when(inner)(inner_passes)
    kv1.arrive("p1b")
    block(1, 128, 128, 768, mask_b, False)

    def edge_passes():
        qd1.on("o1")
        qd0.on("p1")

    pl.when(edge)(edge_passes)
    pl.when(inner)(lambda: qd1.on("p1"))
    kv0.arrive("o3")
    kv0.arrive("o4")
    block(0, 0, 128, ALL, mask_a, False)
    pl.when(edge)(lambda: qd1.on("p1"))
    kv1.arrive("o3")
    kv1.arrive("o4")
    block(1, 0, 128, ALL, mask_a, False)

    st_copies = []
    for k in range(1, RING):
        spot = lax.rem(z + k, RING)
        slot = SLOTS[k - 1]
        digit = 0
        for d in range(RING):
            here = 1 - (spot - d) * (spot - d)
            here = (here + jnp.abs(here)) // 2
            digit = digit + here * (slot // 8**d % 8)
        copy = remote(
            stat.at[:, pl.ds(0, 256)], stat_g.at[digit], st_send.at[k - 1], st_recv.at[k - 1], peers[k - 1]
        )
        copy.start()
        st_copies.append(copy)

    qd0.on("o2")
    qd0.on("p2")

    class Scatter:
        def __init__(self, r):
            self.r = r
            self.copies = []

        def sems(self, i):
            return rs_send.at[self.r, i], rs_recv.at[self.r, i]

        def send(self, i, src, dst, device):
            copy = remote(src, dst, *self.sems(i), device)
            copy.start()
            self.copies.append(copy)

        def arrive(self, i, dst, device):
            remote(dst, dst, *self.sems(i), device).wait_recv()

        def part(self, dx, product):
            r = self.r
            both = product(dx)
            low, high = both[:, 0:COLS], both[:, COLS : 2 * COLS]
            sib_out[r, dx] = jnp.where(core == 0, high, low).astype(BF16)
            self.send(dx, sib_out.at[r, dx], sib_in.at[r, dx], sibling)
            own[r, dx] = jnp.where(core == 0, low, high)

        def pair_sum(self, dx):
            r = self.r
            self.arrive(dx, sib_in.at[r, dx], sibling)
            return own[r, dx] + sib_in[r, dx].astype(F32)

        def halves(self):
            r = self.r
            far[r] = self.pair_sum(2).astype(BF16)
            self.send(4, far.at[r, pl.ds(0, 256)], half_in.at[r, 0], right)
            self.send(5, far.at[r, pl.ds(256, 256)], half_in.at[r, 1], left)

        def direct(self):
            r = self.r
            own[r, 1] = self.pair_sum(1)
            near[r, 0, 256:512] = own[r, 1, 256:512].astype(BF16)
            self.send(6, near.at[r, 0, pl.ds(256, 256)], near_in.at[r, 0, pl.ds(256, 256)], right)
            own[r, 3] = self.pair_sum(3)
            near[r, 1, 0:256] = own[r, 3, 0:256].astype(BF16)
            self.send(7, near.at[r, 1, pl.ds(0, 256)], near_in.at[r, 1, pl.ds(0, 256)], left)
            own[r, 0] = self.pair_sum(0)

        def summed(self):
            r = self.r
            self.arrive(4, half_in.at[r, 0], right)
            near[r, 0, 0:256] = (own[r, 1, 0:256] + half_in[r, 0].astype(F32)).astype(BF16)
            self.send(8, near.at[r, 0, pl.ds(0, 256)], near_in.at[r, 0, pl.ds(0, 256)], right)
            self.arrive(5, half_in.at[r, 1], left)
            near[r, 1, 256:512] = (own[r, 3, 256:512] + half_in[r, 1].astype(F32)).astype(BF16)
            self.send(9, near.at[r, 1, pl.ds(256, 256)], near_in.at[r, 1, pl.ds(256, 256)], left)

        def last(self, into):
            r = self.r
            self.arrive(6, near_in.at[r, 0, pl.ds(256, 256)], right)
            self.arrive(7, near_in.at[r, 1, pl.ds(0, 256)], left)
            self.arrive(8, near_in.at[r, 0, pl.ds(0, 256)], right)
            self.arrive(9, near_in.at[r, 1, pl.ds(256, 256)], left)
            into[...] = (own[r, 0] + near_in[r, 0].astype(F32) + near_in[r, 1].astype(F32)).astype(BF16)

        def drain(self):
            for copy in self.copies:
                copy.wait_send()

    def chip_span(dx):
        return pl.ds(pl.multiple_of(lax.rem(x + dx, 4) * 2 * COLS, 2 * COLS), 2 * COLS)

    for h in range(HEADS):
        att[:, h * 128 : (h + 1) * 128] = nn(unperm[h], att_p[h]).astype(BF16)
    scatter_out = Scatter(0)

    def forward_part(dx):
        scatter_out.part(dx, lambda dx: nn(att[...], wo[:, chip_span(dx)]))

    forward_part(2)
    qd1.on("o2")
    qd1.on("p2")
    qd0.send("p1b")
    qd1.send("p1b")
    forward_part(1)
    forward_part(3)
    scatter_out.halves()
    qd0.on("p3")
    forward_part(0)
    scatter_out.direct()
    for h in range(HEADS):
        gq[:, h * 128 : (h + 1) * 128] = nn(unperm[h], dq_p[h]).astype(BF16)
    qd1.on("p3")
    for dx in (2, 1, 3, 0):
        acc[dx] = nt(gq[...], wq[chip_span(dx)])
    for k in range(1, RING):
        remote(
            stat_g.at[0], stat_g.at[0], st_send.at[k - 1], st_recv.at[k - 1], peers[k - 1]
        ).wait_recv()
    quad_stat = jnp.concatenate([stat_g[1, :, 0:128], stat_g[2, :, 0:128]], 1)
    low_lanes = lax.broadcasted_iota(jnp.int32, (8, 128), 1) < 64
    oct_stat = jnp.concatenate(
        [
            jnp.where(low_lanes, stat_g[a, :, 0:128], pltpu.roll(stat_g[a + 1, :, 0:128], 64, 1))
            for a in (3, 5)
        ],
        1,
    )

    def far_block(h, start, depth, stats, mask):
        q_rows, d_rows = qd[h, start : start + 256, first], qd[h, start : start + 256, second]
        top, inv, delta = (stats[i : i + 1] for i in (h, 2 + h, 4 + h))
        p = jnp.exp(nt(kv[h, 0:depth, first], q_rows) - top) * inv
        if mask is not None:
            p = p * mask[...]
        p_low = p.astype(BF16)
        slope = (p * (nt(kv[h, 0:depth, second], d_rows) - delta)).astype(BF16)
        grads[h, 0:depth, first] += nn(slope, q_rows)
        grads[h, 0:depth, second] += nn(p_low, d_rows)

    def to_tokens(h):
        gkv_p[h] = grads[h].astype(BF16)
        gkv[:, h * 256 : (h + 1) * 256] = nn(unperm[h], gkv_p[h]).astype(BF16)

    far_block(0, QUAD0, 128, quad_stat, mask_q)
    far_block(1, QUAD0, 128, quad_stat, mask_q)
    qd0.arrive("p1b")
    far_block(0, PAIR, 256, stat_g[0], mask_p)
    scatter_out.summed()
    qd0.arrive("o3")
    qd0.arrive("o4")
    far_block(0, OCT0, 64, oct_stat, None)
    to_tokens(0)
    qd1.arrive("p1b")
    far_block(1, PAIR, 256, stat_g[0], mask_p)
    qd1.arrive("o3")
    qd1.arrive("o4")
    far_block(1, OCT0, 64, oct_stat, None)
    to_tokens(1)

    scatter_in = Scatter(1)

    def back(dx):
        return acc[dx] + nt(gkv[...], wkv[chip_span(dx)])

    for dx in (2, 1, 3):
        scatter_in.part(dx, back)
    scatter_in.halves()
    scatter_in.part(0, back)
    scatter_in.direct()
    scatter_out.last(out_ref)
    scatter_in.summed()
    scatter_in.last(ing_ref)

    for name in steps:
        for ring in rings:
            ring.sent(name)
    for copy in st_copies:
        copy.wait_send()
    scatter_out.drain()
    scatter_in.drain()


def on_device(tokens, w_qkv, w_out, offsets, cotangent):
    whole = pl.BlockSpec(memory_space=pl.ANY)
    vmem = pl.BlockSpec(memory_space=pltpu.VMEM)
    return pl.pallas_call(
        kernel,
        out_shape=(jax.ShapeDtypeStruct((ROWS, COLS), BF16),) * 2,
        in_specs=[whole] * 5,
        out_specs=(vmem, vmem),
        scratch_shapes=[
            pltpu.VMEM((ROWS, MODEL), BF16),
            pltpu.VMEM((MODEL, 512), BF16),
            pltpu.VMEM((MODEL, 256), BF16),
            pltpu.VMEM((256, MODEL), BF16),
            pltpu.VMEM((ROWS, MODEL), BF16),
            pltpu.SMEM((HEADS,), jnp.int32),
            pltpu.VMEM((ROWS, 512), BF16),
            pltpu.VMEM((HEADS, ALL, 256), BF16),
            pltpu.VMEM((HEADS, ALL, 256), BF16),
            pltpu.VMEM((HEADS, ROWS, ROWS), BF16),
            pltpu.VMEM((HEADS, ROWS, ROWS), BF16),
            pltpu.VMEM((ALL, 128), F32),
            pltpu.VMEM((768, 128), F32),
            pltpu.VMEM((256, 256), F32),
            pltpu.VMEM((128, 256), F32),
            pltpu.VMEM((HEADS, ROWS, 256), F32),
            pltpu.VMEM((HEADS, ROWS, 128), BF16),
            pltpu.VMEM((HEADS, ROWS, 128), BF16),
            pltpu.VMEM((HEADS, ROWS, 256), BF16),
            pltpu.VMEM((ROWS, 256), BF16),
            pltpu.VMEM((ROWS, 256), BF16),
            pltpu.VMEM((ROWS, 512), BF16),
            pltpu.VMEM((4, ROWS, 2 * COLS), F32),
            pltpu.VMEM((8, ROWS), F32),
            pltpu.VMEM((7, 8, 256), F32),
            pltpu.VMEM((2, 4, ROWS, COLS), F32),
            pltpu.VMEM((2, 4, ROWS, COLS), BF16),
            pltpu.VMEM((2, 4, ROWS, COLS), BF16),
            pltpu.VMEM((2, ROWS, COLS), BF16),
            pltpu.VMEM((2, 2, 256, COLS), BF16),
            pltpu.VMEM((2, 2, ROWS, COLS), BF16),
            pltpu.VMEM((2, 2, ROWS, COLS), BF16),
            pltpu.SemaphoreType.DMA((9,)),
            pltpu.SemaphoreType.DMA((2, HEADS, 8)),
            pltpu.SemaphoreType.DMA((2, HEADS, 8)),
            pltpu.SemaphoreType.DMA((7,)),
            pltpu.SemaphoreType.DMA((7,)),
            pltpu.SemaphoreType.DMA((2, 10)),
            pltpu.SemaphoreType.DMA((2, 10)),
        ],
        compiler_params=pltpu.CompilerParams(
            collective_id=0, has_side_effects=True, vmem_limit_bytes=52 * 1024 * 1024 + 512 * 1024
        ),
    )(tokens, w_qkv, w_out, offsets, cotangent)


def solution(mesh):
    in_specs = (P("seq", None), P(None, None, "head"), P("head", None), P("head"), P("seq", None))
    out_specs = (P("seq", "head"), P("seq", "head"))
    return jax.shard_map(on_device, mesh=mesh, in_specs=in_specs, out_specs=out_specs, check_vma=False)
```

```python
import math

import jax
import jax.numpy as jnp
from jax import lax
from jax.experimental import pallas as pl
from jax.experimental.pallas import tpu as pltpu
from jax.sharding import PartitionSpec as P

MESH = pl.DeviceIdType.MESH
F32, BF16 = jnp.float32, jnp.bfloat16
ROWS = 512
MODEL = 2048
HD = 128
HEADS = 2
RING = 8
ALL = 1280
PAIR, QUAD0, QUAD1, OCT0, OCT1, OCT2, OCT3 = 512, 768, 896, 1024, 1088, 1152, 1216
COLS = 256
NEG = float("-inf")


def nn(a, b):
    return jnp.dot(a, b, preferred_element_type=F32)


def nt(a, b):
    return lax.dot_general(a, b, (((1,), (1,)), ((), ())), preferred_element_type=F32)


def tn(a, b):
    return lax.dot_general(a, b, (((0,), (0,)), ((), ())), preferred_element_type=F32)


def slot_table():
    tables = []
    for k in range(1, RING):
        code = 0
        for d in range(RING):
            source = (d - k) % RING
            inner = d % 4 in (1, 2)
            side = 1 if d % 2 == 1 else -1
            out_dist = (source - d) * side % RING
            in_dist = (d - source) * side % RING
            if source // 2 == d // 2:
                slot = 0
            elif source // 4 == d // 4:
                slot = 1 if source % 4 in (1, 2) else 2
            elif inner:
                slot = {2: 3, 3: 4}[in_dist] if in_dist in (2, 3) else {3: 5, 4: 6}[out_dist]
            else:
                slot = 2 + out_dist
            code += slot * 8**d
        tables.append(code)
    return tables


SLOTS = slot_table()


def kernel(
    tok_hbm, wqkv_hbm, wo_hbm, off_hbm, cot_hbm, both_ref,
    tok, wkv, wq, wo, cot, off_ref, raw, kv, qd, perm, unperm, mask_a, mask_b, mask_p, mask_q,
    grads, keep_a, keep_b, keep_c, att_p, dq_p, gkv_p, att, gq, gkv, acc, stat, stat_g,
    own, sib_out, sib_in, far, half_in, near, near_in,
    load_sem, ring_send, ring_recv, st_send, st_recv, rs_send, rs_recv, turn_sem,
):
    seq = lax.axis_index("seq")
    head = lax.axis_index("head")
    z = lax.rem(seq, RING)
    base = seq - z
    odd = lax.rem(z, 2)
    partner = (base + z + 1 - 2 * odd, head)
    outer = (base + lax.rem(z + 2 * odd + RING - 1, RING), head)
    inner = lax.rem((lax.rem(z, 4) + 1) // 2, 2) == 1
    edge = jnp.logical_not(inner)
    x, core = head // 2, lax.rem(head, 2)
    sibling = (seq, head + 1 - 2 * core)
    right = (seq, lax.rem(x + 1, 4) * 2 + core)
    left = (seq, lax.rem(x + 3, 4) * 2 + core)

    loads = [
        pltpu.make_async_copy(off_hbm, off_ref, load_sem.at[0]),
        pltpu.make_async_copy(tok_hbm, tok, load_sem.at[1]),
    ]
    for h in range(HEADS):
        for part in range(2):
            loads.append(
                pltpu.make_async_copy(
                    wqkv_hbm.at[1 + part, :, pl.ds(h * 128, 128)],
                    wkv.at[:, pl.ds(h * 256 + part * 128, 128)],
                    load_sem.at[2 + 2 * h + part],
                )
            )
    late_loads = [
        pltpu.make_async_copy(wqkv_hbm.at[0], wq, load_sem.at[6]),
        pltpu.make_async_copy(cot_hbm, cot, load_sem.at[7]),
        pltpu.make_async_copy(wo_hbm, wo, load_sem.at[8]),
    ]
    for copy in loads:
        copy.start()

    barrier = pltpu.get_barrier_semaphore()
    peers = [(base + lax.rem(z + k, RING), head) for k in range(1, RING)]
    for device in peers + [sibling, right, left]:
        pl.semaphore_signal(barrier, inc=1, device_id=device, device_id_type=MESH)

    index = lax.broadcasted_iota(jnp.int32, (ROWS, 128), 0)
    lane = lax.broadcasted_iota(jnp.int32, (ROWS, 128), 1)

    def levels(key, query, start):
        far_end = jnp.maximum(key, query)
        count = jnp.full(key.shape, float(start), F32)
        for limit in (256, 128, 64):
            count = count + jnp.where(far_end < limit, 1.0, 0.0)
        return count

    mask_a[0:512] = levels(index, lane, 1)
    mask_a[512:768] = levels(index[0:256], lane[0:256], 0)
    quad_mask = levels(index[0:128], lane[0:128], -1)
    mask_a[768:896] = quad_mask
    mask_a[896:1024] = quad_mask
    mask_a[1024:1280] = jnp.where(lane[0:256] < 64, 1.0, 0.0)
    mask_b[0:512] = levels(index, lane + 128, 1)
    mask_b[512:768] = levels(index[0:256], lane[0:256] + 128, 0)
    mask_p[:, 0:128] = levels(index[0:256], lane[0:256], 0)
    mask_p[:, 128:256] = levels(index[0:256], lane[0:256] + 128, 0)
    mask_q[:, 0:128] = quad_mask
    mask_q[:, 128:256] = quad_mask
    for copy in late_loads:
        copy.start()

    loads[0].wait()
    for h in range(HEADS):
        offset = off_ref[h]
        block = index >> 6
        turned = ((block & 1) << 2) | (block & 2) | (block >> 2)
        old = ((index & 63) << 3) + ((turned + offset) & 7)
        rest = ((index & 7) - offset) & 7
        new = ((((rest & 1) << 2) | (rest & 2) | (rest >> 2)) << 6) + (index >> 3)
        for c in range(ROWS // 128):
            perm[h, :, c * 128 : (c + 1) * 128] = jnp.where(old == lane + c * 128, 1.0, 0.0).astype(BF16)
            unperm[h, :, c * 128 : (c + 1) * 128] = jnp.where(new == lane + c * 128, 1.0, 0.0).astype(BF16)

    def remote(src, dst, send, recv, device):
        return pltpu.make_async_remote_copy(
            src_ref=src, dst_ref=dst, send_sem=send, recv_sem=recv, device_id=device, device_id_type=MESH
        )

    steps = {
        "p1": ((0, 128, PAIR), (0, 128, PAIR), partner),
        "p1b": ((128, 128, PAIR + 128), (128, 128, PAIR + 128), partner),
        "o1": ((0, 128, QUAD0), (0, 64, OCT0), outer),
        "o2": ((PAIR, 128, QUAD1), (PAIR, 64, OCT1), outer),
        "p2": ((QUAD0, 128, QUAD0), (OCT0, 64, OCT0), partner),
        "o3": ((OCT0, 64, OCT2), (QUAD0, 64, OCT2), outer),
        "p3": ((QUAD1, 128, QUAD1), (OCT1, 64, OCT1), partner),
        "o4": ((OCT1, 64, OCT3), (QUAD1, 64, OCT3), outer),
    }
    arrivals = {
        "p1": ((PAIR, 128), (PAIR, 128)),
        "p1b": ((PAIR + 128, 128), (PAIR + 128, 128)),
        "o1": ((QUAD0, 128), (OCT0, 64)),
        "o2": ((QUAD1, 128), (OCT1, 64)),
        "p2": ((OCT0, 64), (QUAD0, 128)),
        "o3": ((OCT2, 64), (OCT2, 64)),
        "p3": ((OCT1, 64), (QUAD1, 128)),
        "o4": ((OCT3, 64), (OCT3, 64)),
    }
    order = {name: i for i, name in enumerate(steps)}
    onward = {"o1": "p2", "p1": "o2", "o2": "p3", "p2": "o3", "p3": "o4"}

    class Gather:
        def __init__(self, buf, send, recv):
            self.buf, self.send_sem, self.recv_sem = buf, send, recv

        def each(self, name, act):
            in_case, edge_case, device = steps[name]
            if in_case == edge_case:
                act(in_case, device)
            else:
                pl.when(inner)(lambda: act(in_case, device))
                pl.when(edge)(lambda: act(edge_case, device))

        def copy(self, name, case, device):
            src, rows, dst = case
            i = order[name]
            return remote(
                self.buf.at[pl.ds(src, rows)], self.buf.at[pl.ds(dst, rows)],
                self.send_sem.at[i], self.recv_sem.at[i], device,
            )

        def send(self, name):
            self.each(name, lambda case, device: self.copy(name, case, device).start())

        def sent(self, name):
            self.each(name, lambda case, device: self.copy(name, case, device).wait_send())

        def arrive(self, name):
            i, device = order[name], steps[name][2]

            def act(case):
                spot = self.buf.at[pl.ds(case[0], case[1])]
                remote(spot, spot, self.send_sem.at[i], self.recv_sem.at[i], device).wait_recv()

            in_case, edge_case = arrivals[name]
            if in_case == edge_case:
                act(in_case)
            else:
                pl.when(inner)(lambda: act(in_case))
                pl.when(edge)(lambda: act(edge_case))

        def own(self):
            self.send("o1")
            self.send("p1")

        def on(self, name):
            self.arrive(name)
            self.send(onward[name])

    rings = [Gather(buf.at[h], ring_send.at[i, h], ring_recv.at[i, h]) for i, buf in enumerate((kv, qd)) for h in range(HEADS)]
    kv0, kv1, qd0, qd1 = rings

    for copy in loads[1:]:
        copy.wait()
    raw[...] = nn(tok[...], wkv[...]).astype(BF16)
    kv[0, 0:ROWS] = nn(perm[0], raw[:, 0:256]).astype(BF16)
    pl.semaphore_wait(barrier, len(peers) + 3)
    pl.when(core == 1)(lambda: pl.semaphore_wait(turn_sem, 1))
    kv0.own()
    pl.when(core == 0)(lambda: pl.semaphore_signal(turn_sem, inc=1, device_id=sibling, device_id_type=MESH))
    kv[1, 0:ROWS] = nn(perm[1], raw[:, 256:512]).astype(BF16)
    kv1.own()
    late_loads[0].wait()
    queries = (nn(tok[...], wq[...]) * (1.0 / math.sqrt(HD))).astype(BF16)
    late_loads[1].wait()
    late_loads[2].wait()
    upstream = nt(cot[...], wo[...]).astype(BF16)
    for h in range(HEADS):
        raw[:, h * 256 : h * 256 + 128] = queries[:, h * 128 : (h + 1) * 128]
        raw[:, h * 256 + 128 : h * 256 + 256] = upstream[:, h * 128 : (h + 1) * 128]
    kv0.on("p1")
    kv0.on("o1")
    pl.when(edge)(lambda: kv0.send("p1b"))
    for h in range(HEADS):
        qd[h, 0:ROWS] = nn(perm[h], raw[:, h * 256 : (h + 1) * 256]).astype(BF16)
    kv1.on("p1")
    kv1.on("o1")
    pl.when(edge)(lambda: kv1.send("p1b"))

    first, second = slice(0, 128), slice(128, 256)

    def forward(h, start, width, depth, mask, keep):
        q_rows, d_rows = qd[h, start : start + width, first], qd[h, start : start + width, second]
        s = nt(kv[h, 0:depth, first], q_rows)
        if mask is not None:
            s = jnp.where(mask[...] > 0.0, s, NEG)
        top = jnp.max(s, axis=0, keepdims=True)
        e = jnp.exp(s - top)
        if mask is not None:
            e = e * mask[...]
        inv = 1.0 / jnp.sum(e, axis=0, keepdims=True)
        p = e * inv
        if keep is not None:
            keep[...] = p
        attended = tn(p.astype(BF16), kv[h, 0:depth, second]).astype(BF16)
        att_p[h, start : start + width] = attended
        product = d_rows.astype(F32) * attended.astype(F32)
        delta = jnp.sum(product.T, axis=0, keepdims=True)
        stat[h : h + 1, start : start + width] = top
        stat[2 + h : 3 + h, start : start + width] = inv
        stat[4 + h : 5 + h, start : start + width] = delta
        return p, delta

    def backward(h, start, width, depth, p, delta, fresh):
        q_rows, d_rows = qd[h, start : start + width, first], qd[h, start : start + width, second]
        slope = (p * (nt(kv[h, 0:depth, second], d_rows) - delta)).astype(BF16)
        dq_p[h, start : start + width] = (tn(slope, kv[h, 0:depth, first]) * (1.0 / math.sqrt(HD))).astype(BF16)
        dk = nn(slope[0:ROWS], q_rows)
        dv = nn(p[0:ROWS].astype(BF16), d_rows)
        if fresh:
            grads[h, :, first] = dk
            grads[h, :, second] = dv
        else:
            grads[h, :, first] += dk
            grads[h, :, second] += dv

    def block(h, start, width, depth, mask, fresh):
        p, delta = forward(h, start, width, depth, mask, None)
        backward(h, start, width, depth, p, delta, fresh)

    forward(0, 256, 256, ROWS, None, keep_c.at[0])
    kv0.on("o2")
    forward(1, 256, 256, ROWS, None, keep_c.at[1])
    kv1.on("o2")
    kv0.on("p2")
    kv1.on("p2")

    def pair_rest(low, high):
        low.send("p1b")
        high.send("p1b")

    def query_own():
        qd0.own()
        qd1.own()

    def edge_own():
        query_own()
        pair_rest(qd0, qd1)

    pl.when(inner)(lambda: pair_rest(kv0, kv1))
    pl.when(edge)(edge_own)
    backward(0, 256, 256, ROWS, keep_c[0], stat[4:5, 256:512], True)
    kv0.on("p3")
    backward(1, 256, 256, ROWS, keep_c[1], stat[5:6, 256:512], True)
    kv1.on("p3")
    pl.when(inner)(query_own)
    kv0.arrive("p1b")
    block(0, 128, 128, 768, mask_b, False)
    kv0.arrive("o3")
    kv0.arrive("o4")

    def inner_passes(ring):
        ring.on("o1")
        ring.on("p1")

    forward(0, 0, 128, ALL, mask_a, keep_a.at[0])
    pl.when(inner)(lambda: inner_passes(qd0))
    kv1.arrive("p1b")
    forward(1, 128, 128, 768, mask_b, keep_b)
    kv1.arrive("o3")
    kv1.arrive("o4")
    pl.when(inner)(lambda: inner_passes(qd1))

    def edge_passes():
        qd0.on("p1")
        qd0.on("o1")

    pl.when(edge)(edge_passes)
    forward(1, 0, 128, ALL, mask_a, keep_a.at[1])

    st_copies = []
    for k in range(1, RING):
        spot = lax.rem(z + k, RING)
        slot = SLOTS[k - 1]
        digit = 0
        for d in range(RING):
            here = 1 - (spot - d) * (spot - d)
            here = (here + jnp.abs(here)) // 2
            digit = digit + here * (slot // 8**d % 8)
        copy = remote(
            stat.at[:, pl.ds(0, 256)], stat_g.at[digit], st_send.at[k - 1], st_recv.at[k - 1], peers[k - 1]
        )
        copy.start()
        st_copies.append(copy)

    pl.when(inner)(lambda: qd0.on("o2"))
    pl.when(edge)(lambda: qd1.on("o1"))

    class Scatter:
        def __init__(self, r):
            self.r = r
            self.copies = []

        def sems(self, i):
            return rs_send.at[self.r, i], rs_recv.at[self.r, i]

        def send(self, i, src, dst, device):
            copy = remote(src, dst, *self.sems(i), device)
            copy.start()
            self.copies.append(copy)

        def arrive(self, i, dst, device):
            remote(dst, dst, *self.sems(i), device).wait_recv()

        def part(self, dx, product):
            r = self.r
            both = product(dx)
            low, high = both[:, 0:COLS], both[:, COLS : 2 * COLS]
            sib_out[r, dx] = jnp.where(core == 0, high, low).astype(BF16)
            self.send(dx, sib_out.at[r, dx], sib_in.at[r, dx], sibling)
            own[r, dx] = jnp.where(core == 0, low, high)

        def pair_sum(self, dx):
            r = self.r
            self.arrive(dx, sib_in.at[r, dx], sibling)
            return own[r, dx] + sib_in[r, dx].astype(F32)

        def halves(self):
            r = self.r
            far[r] = self.pair_sum(2).astype(BF16)
            self.send(4, far.at[r, pl.ds(0, 256)], half_in.at[r, 0], right)
            self.send(5, far.at[r, pl.ds(256, 256)], half_in.at[r, 1], left)

        def direct(self):
            r = self.r
            own[r, 1] = self.pair_sum(1)
            near[r, 0, 256:512] = own[r, 1, 256:512].astype(BF16)
            self.send(6, near.at[r, 0, pl.ds(256, 256)], near_in.at[r, 0, pl.ds(256, 256)], right)
            own[r, 3] = self.pair_sum(3)
            near[r, 1, 0:256] = own[r, 3, 0:256].astype(BF16)
            self.send(7, near.at[r, 1, pl.ds(0, 256)], near_in.at[r, 1, pl.ds(0, 256)], left)

        def summed(self):
            r = self.r
            self.arrive(4, half_in.at[r, 0], right)
            near[r, 0, 0:256] = (own[r, 1, 0:256] + half_in[r, 0].astype(F32)).astype(BF16)
            self.send(8, near.at[r, 0, pl.ds(0, 256)], near_in.at[r, 0, pl.ds(0, 256)], right)
            self.arrive(5, half_in.at[r, 1], left)
            near[r, 1, 256:512] = (own[r, 3, 256:512] + half_in[r, 1].astype(F32)).astype(BF16)
            self.send(9, near.at[r, 1, pl.ds(256, 256)], near_in.at[r, 1, pl.ds(256, 256)], left)

        def last(self, into):
            r = self.r
            mine = self.pair_sum(0)
            self.arrive(6, near_in.at[r, 0, pl.ds(256, 256)], right)
            self.arrive(7, near_in.at[r, 1, pl.ds(0, 256)], left)
            self.arrive(8, near_in.at[r, 0, pl.ds(0, 256)], right)
            self.arrive(9, near_in.at[r, 1, pl.ds(256, 256)], left)
            into[...] = (mine + near_in[r, 0].astype(F32) + near_in[r, 1].astype(F32)).astype(BF16)

        def drain(self):
            for copy in self.copies:
                copy.wait_send()

    def chip_span(dx):
        return pl.ds(pl.multiple_of(lax.rem(x + dx, 4) * 2 * COLS, 2 * COLS), 2 * COLS)

    for h in range(HEADS):
        att[:, h * 128 : (h + 1) * 128] = nn(unperm[h], att_p[h]).astype(BF16)
    scatter_out = Scatter(0)

    def forward_part(dx):
        scatter_out.part(dx, lambda dx: nn(att[...], wo[:, chip_span(dx)]))

    forward_part(2)
    pl.when(edge)(lambda: qd1.on("p1"))
    forward_part(1)

    def inner_more():
        qd1.on("o2")
        pair_rest(qd0, qd1)

    pl.when(inner)(inner_more)
    scatter_out.halves()
    forward_part(3)
    forward_part(0)
    qd0.on("p2")
    backward(1, 128, 128, 768, keep_b[...], stat[5:6, 128:256], False)
    pl.when(edge)(lambda: qd0.on("o2"))
    backward(0, 0, 128, ALL, keep_a[0], stat[4:5, 0:128], False)
    qd1.on("p2")
    pl.when(edge)(lambda: qd1.on("o2"))
    backward(1, 0, 128, ALL, keep_a[1], stat[5:6, 0:128], False)
    scatter_out.direct()
    qd0.on("p3")
    for k in range(1, RING):
        remote(
            stat_g.at[0], stat_g.at[0], st_send.at[k - 1], st_recv.at[k - 1], peers[k - 1]
        ).wait_recv()
    quad_stat = jnp.concatenate([stat_g[1, :, 0:128], stat_g[2, :, 0:128]], 1)
    low_lanes = lax.broadcasted_iota(jnp.int32, (8, 128), 1) < 64
    oct_stat = jnp.concatenate(
        [
            jnp.where(low_lanes, stat_g[a, :, 0:128], pltpu.roll(stat_g[a + 1, :, 0:128], 64, 1))
            for a in (3, 5)
        ],
        1,
    )

    def far_block(h, start, depth, stats, mask):
        q_rows, d_rows = qd[h, start : start + 256, first], qd[h, start : start + 256, second]
        top, inv, delta = (stats[i : i + 1] for i in (h, 2 + h, 4 + h))
        p = jnp.exp(nt(kv[h, 0:depth, first], q_rows) - top) * inv
        if mask is not None:
            p = p * mask[...]
        p_low = p.astype(BF16)
        slope = (p * (nt(kv[h, 0:depth, second], d_rows) - delta)).astype(BF16)
        grads[h, 0:depth, first] += nn(slope, q_rows)
        grads[h, 0:depth, second] += nn(p_low, d_rows)

    def to_tokens(h):
        gkv_p[h] = grads[h].astype(BF16)
        gkv[:, h * 256 : (h + 1) * 256] = nn(unperm[h], gkv_p[h]).astype(BF16)

    far_block(0, QUAD0, 128, quad_stat, mask_q)
    for h in range(HEADS):
        gq[:, h * 128 : (h + 1) * 128] = nn(unperm[h], dq_p[h]).astype(BF16)
    qd1.on("p3")
    for dx in (2, 1, 3, 0):
        acc[dx] = nt(gq[...], wq[chip_span(dx)])
    far_block(1, QUAD0, 128, quad_stat, mask_q)
    qd0.arrive("p1b")
    far_block(0, PAIR, 256, stat_g[0], mask_p)
    scatter_out.summed()
    qd0.arrive("o3")
    qd0.arrive("o4")
    far_block(0, OCT0, 64, oct_stat, None)
    to_tokens(0)
    qd1.arrive("p1b")
    far_block(1, PAIR, 256, stat_g[0], mask_p)
    qd1.arrive("o3")
    qd1.arrive("o4")
    far_block(1, OCT0, 64, oct_stat, None)
    to_tokens(1)

    scatter_in = Scatter(1)

    def back(dx):
        return acc[dx] + nt(gkv[...], wkv[chip_span(dx)])

    for dx in (2, 1):
        scatter_in.part(dx, back)
    scatter_in.halves()
    scatter_in.part(3, back)
    scatter_in.direct()
    scatter_in.part(0, back)
    scatter_out.last(both_ref.at[0])
    scatter_in.summed()
    scatter_in.last(both_ref.at[1])

    for name in steps:
        for ring in rings:
            ring.sent(name)
    for copy in st_copies:
        copy.wait_send()
    scatter_out.drain()
    scatter_in.drain()


def on_device(tokens, w_qkv, w_out, offsets, cotangent):
    whole = pl.BlockSpec(memory_space=pl.ANY)
    vmem = pl.BlockSpec(memory_space=pltpu.VMEM)
    both = pl.pallas_call(
        kernel,
        out_shape=jax.ShapeDtypeStruct((2, ROWS, COLS), BF16),
        in_specs=[whole] * 5,
        out_specs=vmem,
        scratch_shapes=[
            pltpu.VMEM((ROWS, MODEL), BF16),
            pltpu.VMEM((MODEL, 512), BF16),
            pltpu.VMEM((MODEL, 256), BF16),
            pltpu.VMEM((256, MODEL), BF16),
            pltpu.VMEM((ROWS, MODEL), BF16),
            pltpu.SMEM((HEADS,), jnp.int32),
            pltpu.VMEM((ROWS, 512), BF16),
            pltpu.VMEM((HEADS, ALL, 256), BF16),
            pltpu.VMEM((HEADS, ALL, 256), BF16),
            pltpu.VMEM((HEADS, ROWS, ROWS), BF16),
            pltpu.VMEM((HEADS, ROWS, ROWS), BF16),
            pltpu.VMEM((ALL, 128), F32),
            pltpu.VMEM((768, 128), F32),
            pltpu.VMEM((256, 256), F32),
            pltpu.VMEM((128, 256), F32),
            pltpu.VMEM((HEADS, ROWS, 256), F32),
            pltpu.VMEM((HEADS, ALL, 128), F32),
            pltpu.VMEM((768, 128), F32),
            pltpu.VMEM((HEADS, ROWS, 256), F32),
            pltpu.VMEM((HEADS, ROWS, 128), BF16),
            pltpu.VMEM((HEADS, ROWS, 128), BF16),
            pltpu.VMEM((HEADS, ROWS, 256), BF16),
            pltpu.VMEM((ROWS, 256), BF16),
            pltpu.VMEM((ROWS, 256), BF16),
            pltpu.VMEM((ROWS, 512), BF16),
            pltpu.VMEM((4, ROWS, 2 * COLS), F32),
            pltpu.VMEM((8, ROWS), F32),
            pltpu.VMEM((7, 8, 256), F32),
            pltpu.VMEM((2, 4, ROWS, COLS), F32),
            pltpu.VMEM((2, 4, ROWS, COLS), BF16),
            pltpu.VMEM((2, 4, ROWS, COLS), BF16),
            pltpu.VMEM((2, ROWS, COLS), BF16),
            pltpu.VMEM((2, 2, 256, COLS), BF16),
            pltpu.VMEM((2, 2, ROWS, COLS), BF16),
            pltpu.VMEM((2, 2, ROWS, COLS), BF16),
            pltpu.SemaphoreType.DMA((9,)),
            pltpu.SemaphoreType.DMA((2, HEADS, 8)),
            pltpu.SemaphoreType.DMA((2, HEADS, 8)),
            pltpu.SemaphoreType.DMA((7,)),
            pltpu.SemaphoreType.DMA((7,)),
            pltpu.SemaphoreType.DMA((2, 10)),
            pltpu.SemaphoreType.DMA((2, 10)),
            pltpu.SemaphoreType.REGULAR,
        ],
        compiler_params=pltpu.CompilerParams(
            collective_id=0, has_side_effects=True, vmem_limit_bytes=52 * 1024 * 1024 + 512 * 1024
        ),
    )(tokens, w_qkv, w_out, offsets, cotangent)
    return (both[0], both[1])


def solution(mesh):
    in_specs = (P("seq", None), P(None, None, "head"), P("head", None), P("head"), P("seq", None))
    out_specs = (P("seq", "head"), P("seq", "head"))
    return jax.shard_map(on_device, mesh=mesh, in_specs=in_specs, out_specs=out_specs, check_vma=False)
```

```python
import math

import jax
import jax.numpy as jnp
from jax import lax
from jax.experimental import pallas as pl
from jax.experimental.pallas import tpu as pltpu
from jax.sharding import PartitionSpec as P

MESH = pl.DeviceIdType.MESH
F32, BF16 = jnp.float32, jnp.bfloat16
ROWS = 512
MODEL = 2048
HD = 128
HEADS = 2
RING = 8
ALL = 1280
PAIR, QUAD0, QUAD1, OCT0, OCT1, OCT2, OCT3 = 512, 768, 896, 1024, 1088, 1152, 1216
COLS = 256
NEG = float("-inf")


def nn(a, b):
    return jnp.dot(a, b, preferred_element_type=F32)


def nt(a, b):
    return lax.dot_general(a, b, (((1,), (1,)), ((), ())), preferred_element_type=F32)


def tn(a, b):
    return lax.dot_general(a, b, (((0,), (0,)), ((), ())), preferred_element_type=F32)


def slot_table():
    tables = []
    for k in range(1, RING):
        code = 0
        for d in range(RING):
            source = (d - k) % RING
            inner = d % 4 in (1, 2)
            side = 1 if d % 2 == 1 else -1
            out_dist = (source - d) * side % RING
            in_dist = (d - source) * side % RING
            if source // 2 == d // 2:
                slot = 0
            elif source // 4 == d // 4:
                slot = 1 if source % 4 in (1, 2) else 2
            elif inner:
                slot = {2: 3, 3: 4}[in_dist] if in_dist in (2, 3) else {3: 5, 4: 6}[out_dist]
            else:
                slot = 2 + out_dist
            code += slot * 8**d
        tables.append(code)
    return tables


SLOTS = slot_table()


def kernel(
    tok_hbm, wqkv_hbm, wo_hbm, off_hbm, cot_hbm, both_ref,
    tok, wkv, wq, wo, cot, off_ref, raw, kv, qd, perm, unperm, mask_a, mask_b, mask_p, mask_q,
    grads, att_p, dq_p, gkv_p, att, gq, gkv, acc, stat, stat_g,
    own, sib_out, sib_in, far, half_in, near, near_in,
    load_sem, ring_send, ring_recv, st_send, st_recv, rs_send, rs_recv,
):
    seq = lax.axis_index("seq")
    head = lax.axis_index("head")
    z = lax.rem(seq, RING)
    base = seq - z
    odd = lax.rem(z, 2)
    partner = (base + z + 1 - 2 * odd, head)
    outer = (base + lax.rem(z + 2 * odd + RING - 1, RING), head)
    inner = lax.rem((lax.rem(z, 4) + 1) // 2, 2) == 1
    edge = jnp.logical_not(inner)
    x, core = head // 2, lax.rem(head, 2)
    sibling = (seq, head + 1 - 2 * core)
    right = (seq, lax.rem(x + 1, 4) * 2 + core)
    left = (seq, lax.rem(x + 3, 4) * 2 + core)

    loads = [
        pltpu.make_async_copy(off_hbm, off_ref, load_sem.at[0]),
        pltpu.make_async_copy(tok_hbm, tok, load_sem.at[1]),
    ]
    for h in range(HEADS):
        for part in range(2):
            loads.append(
                pltpu.make_async_copy(
                    wqkv_hbm.at[1 + part, :, pl.ds(h * 128, 128)],
                    wkv.at[:, pl.ds(h * 256 + part * 128, 128)],
                    load_sem.at[2 + 2 * h + part],
                )
            )
    late_loads = [
        pltpu.make_async_copy(wqkv_hbm.at[0], wq, load_sem.at[6]),
        pltpu.make_async_copy(cot_hbm, cot, load_sem.at[7]),
        pltpu.make_async_copy(wo_hbm, wo, load_sem.at[8]),
    ]
    for copy in loads:
        copy.start()

    barrier = pltpu.get_barrier_semaphore()
    peers = [(base + lax.rem(z + k, RING), head) for k in range(1, RING)]
    for device in peers + [sibling, right, left]:
        pl.semaphore_signal(barrier, inc=1, device_id=device, device_id_type=MESH)

    index = lax.broadcasted_iota(jnp.int32, (ROWS, 128), 0)
    lane = lax.broadcasted_iota(jnp.int32, (ROWS, 128), 1)

    def levels(key, query, start):
        far_end = jnp.maximum(key, query)
        count = jnp.full(key.shape, float(start), F32)
        for limit in (256, 128, 64):
            count = count + jnp.where(far_end < limit, 1.0, 0.0)
        return count

    mask_a[0:512] = levels(index, lane, 1)
    mask_a[512:768] = levels(index[0:256], lane[0:256], 0)
    quad_mask = levels(index[0:128], lane[0:128], -1)
    mask_a[768:896] = quad_mask
    mask_a[896:1024] = quad_mask
    mask_a[1024:1280] = jnp.where(lane[0:256] < 64, 1.0, 0.0)
    mask_b[0:512] = levels(index, lane + 128, 1)
    mask_b[512:768] = levels(index[0:256], lane[0:256] + 128, 0)
    mask_p[:, 0:128] = levels(index[0:256], lane[0:256], 0)
    mask_p[:, 128:256] = levels(index[0:256], lane[0:256] + 128, 0)
    mask_q[:, 0:128] = quad_mask
    mask_q[:, 128:256] = quad_mask
    for copy in late_loads:
        copy.start()

    loads[0].wait()
    for h in range(HEADS):
        offset = off_ref[h]
        block = index >> 6
        turned = ((block & 1) << 2) | (block & 2) | (block >> 2)
        old = ((index & 63) << 3) + ((turned + offset) & 7)
        rest = ((index & 7) - offset) & 7
        new = ((((rest & 1) << 2) | (rest & 2) | (rest >> 2)) << 6) + (index >> 3)
        for c in range(ROWS // 128):
            perm[h, :, c * 128 : (c + 1) * 128] = jnp.where(old == lane + c * 128, 1.0, 0.0).astype(BF16)
            unperm[h, :, c * 128 : (c + 1) * 128] = jnp.where(new == lane + c * 128, 1.0, 0.0).astype(BF16)

    def remote(src, dst, send, recv, device):
        return pltpu.make_async_remote_copy(
            src_ref=src, dst_ref=dst, send_sem=send, recv_sem=recv, device_id=device, device_id_type=MESH
        )

    steps = {
        "p1": ((0, 128, PAIR), (0, 128, PAIR), partner),
        "p1b": ((128, 128, PAIR + 128), (128, 128, PAIR + 128), partner),
        "o1": ((0, 128, QUAD0), (0, 64, OCT0), outer),
        "o2": ((PAIR, 128, QUAD1), (PAIR, 64, OCT1), outer),
        "p2": ((QUAD0, 128, QUAD0), (OCT0, 64, OCT0), partner),
        "o3": ((OCT0, 64, OCT2), (QUAD0, 64, OCT2), outer),
        "p3": ((QUAD1, 128, QUAD1), (OCT1, 64, OCT1), partner),
        "o4": ((OCT1, 64, OCT3), (QUAD1, 64, OCT3), outer),
    }
    arrivals = {
        "p1": ((PAIR, 128), (PAIR, 128)),
        "p1b": ((PAIR + 128, 128), (PAIR + 128, 128)),
        "o1": ((QUAD0, 128), (OCT0, 64)),
        "o2": ((QUAD1, 128), (OCT1, 64)),
        "p2": ((OCT0, 64), (QUAD0, 128)),
        "o3": ((OCT2, 64), (OCT2, 64)),
        "p3": ((OCT1, 64), (QUAD1, 128)),
        "o4": ((OCT3, 64), (OCT3, 64)),
    }
    order = {name: i for i, name in enumerate(steps)}
    onward = {"o1": "p2", "p1": "o2", "o2": "p3", "p2": "o3", "p3": "o4"}

    class Gather:
        def __init__(self, buf, send, recv):
            self.buf, self.send_sem, self.recv_sem = buf, send, recv

        def each(self, name, act):
            in_case, edge_case, device = steps[name]
            if in_case == edge_case:
                act(in_case, device)
            else:
                pl.when(inner)(lambda: act(in_case, device))
                pl.when(edge)(lambda: act(edge_case, device))

        def copy(self, name, case, device):
            src, rows, dst = case
            i = order[name]
            return remote(
                self.buf.at[pl.ds(src, rows)], self.buf.at[pl.ds(dst, rows)],
                self.send_sem.at[i], self.recv_sem.at[i], device,
            )

        def send(self, name):
            self.each(name, lambda case, device: self.copy(name, case, device).start())

        def sent(self, name):
            self.each(name, lambda case, device: self.copy(name, case, device).wait_send())

        def arrive(self, name):
            i, device = order[name], steps[name][2]

            def act(case):
                spot = self.buf.at[pl.ds(case[0], case[1])]
                remote(spot, spot, self.send_sem.at[i], self.recv_sem.at[i], device).wait_recv()

            in_case, edge_case = arrivals[name]
            if in_case == edge_case:
                act(in_case)
            else:
                pl.when(inner)(lambda: act(in_case))
                pl.when(edge)(lambda: act(edge_case))

        def own(self):
            self.send("o1")
            self.send("p1")

        def on(self, name):
            self.arrive(name)
            self.send(onward[name])

    rings = [Gather(buf.at[h], ring_send.at[i, h], ring_recv.at[i, h]) for i, buf in enumerate((kv, qd)) for h in range(HEADS)]
    kv0, kv1, qd0, qd1 = rings

    for copy in loads[1:]:
        copy.wait()
    raw[...] = nn(tok[...], wkv[...]).astype(BF16)
    kv[0, 0:ROWS] = nn(perm[0], raw[:, 0:256]).astype(BF16)
    pl.semaphore_wait(barrier, len(peers) + 3)
    kv0.own()
    kv[1, 0:ROWS] = nn(perm[1], raw[:, 256:512]).astype(BF16)
    late_loads[0].wait()
    queries = (nn(tok[...], wq[...]) * (1.0 / math.sqrt(HD))).astype(BF16)
    kv1.own()
    late_loads[1].wait()
    late_loads[2].wait()
    upstream = nt(cot[...], wo[...]).astype(BF16)
    for h in range(HEADS):
        raw[:, h * 256 : h * 256 + 128] = queries[:, h * 128 : (h + 1) * 128]
        raw[:, h * 256 + 128 : h * 256 + 256] = upstream[:, h * 128 : (h + 1) * 128]
    kv0.on("o1")
    kv0.on("p1")
    kv0.send("p1b")
    for h in range(HEADS):
        qd[h, 0:ROWS] = nn(perm[h], raw[:, h * 256 : (h + 1) * 256]).astype(BF16)

    first, second = slice(0, 128), slice(128, 256)

    def block(h, start, width, depth, mask, fresh):
        q_rows, d_rows = qd[h, start : start + width, first], qd[h, start : start + width, second]
        s = nt(kv[h, 0:depth, first], q_rows)
        if mask is not None:
            s = jnp.where(mask[...] > 0.0, s, NEG)
        top = jnp.max(s, axis=0, keepdims=True)
        e = jnp.exp(s - top)
        if mask is not None:
            e = e * mask[...]
        inv = 1.0 / jnp.sum(e, axis=0, keepdims=True)
        p = e * inv
        p_low = p.astype(BF16)
        attended = tn(p_low, kv[h, 0:depth, second]).astype(BF16)
        att_p[h, start : start + width] = attended
        product = d_rows.astype(F32) * attended.astype(F32)
        delta = jnp.sum(product.T, axis=0, keepdims=True)
        stat[h : h + 1, start : start + width] = top
        stat[2 + h : 3 + h, start : start + width] = inv
        stat[4 + h : 5 + h, start : start + width] = delta
        slope = (p * (nt(kv[h, 0:depth, second], d_rows) - delta)).astype(BF16)
        dq_p[h, start : start + width] = (tn(slope, kv[h, 0:depth, first]) * (1.0 / math.sqrt(HD))).astype(BF16)
        dk = nn(slope[0:ROWS], q_rows)
        dv = nn(p_low[0:ROWS], d_rows)
        if fresh:
            grads[h, :, first] = dk
            grads[h, :, second] = dv
        else:
            grads[h, :, first] += dk
            grads[h, :, second] += dv

    block(0, 256, 256, ROWS, None, True)
    kv1.on("o1")
    kv1.on("p1")
    block(1, 256, 256, ROWS, None, True)
    kv0.on("o2")
    kv0.on("p2")
    kv0.arrive("p1b")
    block(0, 128, 128, 768, mask_b, False)
    kv1.on("o2")
    kv1.send("p1b")
    kv1.on("p2")
    qd0.own()
    qd1.own()
    kv0.on("p3")
    kv1.on("p3")
    qd0.on("o1")

    def inner_passes():
        qd0.on("p1")
        qd1.on("o1")

    pl.when(inner)(inner_passes)
    kv1.arrive("p1b")
    block(1, 128, 128, 768, mask_b, False)

    def edge_passes():
        qd1.on("o1")
        qd0.on("p1")

    pl.when(edge)(edge_passes)
    pl.when(inner)(lambda: qd1.on("p1"))
    kv0.arrive("o3")
    kv0.arrive("o4")
    block(0, 0, 128, ALL, mask_a, False)
    pl.when(edge)(lambda: qd1.on("p1"))
    kv1.arrive("o3")
    kv1.arrive("o4")
    block(1, 0, 128, ALL, mask_a, False)

    st_copies = []
    for k in range(1, RING):
        spot = lax.rem(z + k, RING)
        slot = SLOTS[k - 1]
        digit = 0
        for d in range(RING):
            here = 1 - (spot - d) * (spot - d)
            here = (here + jnp.abs(here)) // 2
            digit = digit + here * (slot // 8**d % 8)
        copy = remote(
            stat.at[:, pl.ds(0, 256)], stat_g.at[digit], st_send.at[k - 1], st_recv.at[k - 1], peers[k - 1]
        )
        copy.start()
        st_copies.append(copy)

    qd0.on("o2")
    qd0.on("p2")

    class Scatter:
        def __init__(self, r):
            self.r = r
            self.copies = []

        def sems(self, i):
            return rs_send.at[self.r, i], rs_recv.at[self.r, i]

        def send(self, i, src, dst, device):
            copy = remote(src, dst, *self.sems(i), device)
            copy.start()
            self.copies.append(copy)

        def arrive(self, i, dst, device):
            remote(dst, dst, *self.sems(i), device).wait_recv()

        def part(self, dx, product):
            r = self.r
            both = product(dx)
            low, high = both[:, 0:COLS], both[:, COLS : 2 * COLS]
            sib_out[r, dx] = jnp.where(core == 0, high, low).astype(BF16)
            self.send(dx, sib_out.at[r, dx], sib_in.at[r, dx], sibling)
            own[r, dx] = jnp.where(core == 0, low, high)

        def pair_sum(self, dx):
            r = self.r
            self.arrive(dx, sib_in.at[r, dx], sibling)
            return own[r, dx] + sib_in[r, dx].astype(F32)

        def halves(self):
            r = self.r
            far[r] = self.pair_sum(2).astype(BF16)
            self.send(4, far.at[r, pl.ds(0, 256)], half_in.at[r, 0], right)
            self.send(5, far.at[r, pl.ds(256, 256)], half_in.at[r, 1], left)

        def direct(self):
            r = self.r
            own[r, 1] = self.pair_sum(1)
            near[r, 0, 256:512] = own[r, 1, 256:512].astype(BF16)
            self.send(6, near.at[r, 0, pl.ds(256, 256)], near_in.at[r, 0, pl.ds(256, 256)], right)
            own[r, 3] = self.pair_sum(3)
            near[r, 1, 0:256] = own[r, 3, 0:256].astype(BF16)
            self.send(7, near.at[r, 1, pl.ds(0, 256)], near_in.at[r, 1, pl.ds(0, 256)], left)

        def summed(self):
            r = self.r
            self.arrive(4, half_in.at[r, 0], right)
            near[r, 0, 0:256] = (own[r, 1, 0:256] + half_in[r, 0].astype(F32)).astype(BF16)
            self.send(8, near.at[r, 0, pl.ds(0, 256)], near_in.at[r, 0, pl.ds(0, 256)], right)
            self.arrive(5, half_in.at[r, 1], left)
            near[r, 1, 256:512] = (own[r, 3, 256:512] + half_in[r, 1].astype(F32)).astype(BF16)
            self.send(9, near.at[r, 1, pl.ds(256, 256)], near_in.at[r, 1, pl.ds(256, 256)], left)

        def last(self, into):
            r = self.r
            mine = self.pair_sum(0)
            self.arrive(6, near_in.at[r, 0, pl.ds(256, 256)], right)
            self.arrive(7, near_in.at[r, 1, pl.ds(0, 256)], left)
            self.arrive(8, near_in.at[r, 0, pl.ds(0, 256)], right)
            self.arrive(9, near_in.at[r, 1, pl.ds(256, 256)], left)
            into[...] = (mine + near_in[r, 0].astype(F32) + near_in[r, 1].astype(F32)).astype(BF16)

        def drain(self):
            for copy in self.copies:
                copy.wait_send()

    def chip_span(dx):
        return pl.ds(pl.multiple_of(lax.rem(x + dx, 4) * 2 * COLS, 2 * COLS), 2 * COLS)

    for h in range(HEADS):
        att[:, h * 128 : (h + 1) * 128] = nn(unperm[h], att_p[h]).astype(BF16)
    scatter_out = Scatter(0)

    def forward_part(dx):
        scatter_out.part(dx, lambda dx: nn(att[...], wo[:, chip_span(dx)]))

    forward_part(2)
    qd1.on("o2")
    qd1.on("p2")
    qd0.send("p1b")
    qd1.send("p1b")
    forward_part(1)
    forward_part(3)
    scatter_out.halves()
    qd0.on("p3")
    forward_part(0)
    scatter_out.direct()
    for h in range(HEADS):
        gq[:, h * 128 : (h + 1) * 128] = nn(unperm[h], dq_p[h]).astype(BF16)
    qd1.on("p3")
    for dx in (2, 1, 3, 0):
        acc[dx] = nt(gq[...], wq[chip_span(dx)])
    for k in range(1, RING):
        remote(
            stat_g.at[0], stat_g.at[0], st_send.at[k - 1], st_recv.at[k - 1], peers[k - 1]
        ).wait_recv()
    quad_stat = jnp.concatenate([stat_g[1, :, 0:128], stat_g[2, :, 0:128]], 1)
    low_lanes = lax.broadcasted_iota(jnp.int32, (8, 128), 1) < 64
    oct_stat = jnp.concatenate(
        [
            jnp.where(low_lanes, stat_g[a, :, 0:128], pltpu.roll(stat_g[a + 1, :, 0:128], 64, 1))
            for a in (3, 5)
        ],
        1,
    )

    def far_block(h, start, depth, stats, mask):
        q_rows, d_rows = qd[h, start : start + 256, first], qd[h, start : start + 256, second]
        top, inv, delta = (stats[i : i + 1] for i in (h, 2 + h, 4 + h))
        p = jnp.exp(nt(kv[h, 0:depth, first], q_rows) - top) * inv
        if mask is not None:
            p = p * mask[...]
        p_low = p.astype(BF16)
        slope = (p * (nt(kv[h, 0:depth, second], d_rows) - delta)).astype(BF16)
        grads[h, 0:depth, first] += nn(slope, q_rows)
        grads[h, 0:depth, second] += nn(p_low, d_rows)

    def to_tokens(h):
        gkv_p[h] = grads[h].astype(BF16)
        gkv[:, h * 256 : (h + 1) * 256] = nn(unperm[h], gkv_p[h]).astype(BF16)

    far_block(0, QUAD0, 128, quad_stat, mask_q)
    far_block(1, QUAD0, 128, quad_stat, mask_q)
    qd0.arrive("p1b")
    far_block(0, PAIR, 256, stat_g[0], mask_p)
    scatter_out.summed()
    qd0.arrive("o3")
    qd0.arrive("o4")
    far_block(0, OCT0, 64, oct_stat, None)
    to_tokens(0)
    qd1.arrive("p1b")
    far_block(1, PAIR, 256, stat_g[0], mask_p)
    qd1.arrive("o3")
    qd1.arrive("o4")
    far_block(1, OCT0, 64, oct_stat, None)
    to_tokens(1)

    scatter_in = Scatter(1)

    def back(dx):
        return acc[dx] + nt(gkv[...], wkv[chip_span(dx)])

    for dx in (2, 1, 3):
        scatter_in.part(dx, back)
    scatter_in.halves()
    scatter_in.part(0, back)
    scatter_in.direct()
    scatter_out.last(both_ref.at[0])
    scatter_in.summed()
    scatter_in.last(both_ref.at[1])

    for name in steps:
        for ring in rings:
            ring.sent(name)
    for copy in st_copies:
        copy.wait_send()
    scatter_out.drain()
    scatter_in.drain()


def on_device(tokens, w_qkv, w_out, offsets, cotangent):
    whole = pl.BlockSpec(memory_space=pl.ANY)
    vmem = pl.BlockSpec(memory_space=pltpu.VMEM)
    both = pl.pallas_call(
        kernel,
        out_shape=jax.ShapeDtypeStruct((2, ROWS, COLS), BF16),
        in_specs=[whole] * 5,
        out_specs=vmem,
        scratch_shapes=[
            pltpu.VMEM((ROWS, MODEL), BF16),
            pltpu.VMEM((MODEL, 512), BF16),
            pltpu.VMEM((MODEL, 256), BF16),
            pltpu.VMEM((256, MODEL), BF16),
            pltpu.VMEM((ROWS, MODEL), BF16),
            pltpu.SMEM((HEADS,), jnp.int32),
            pltpu.VMEM((ROWS, 512), BF16),
            pltpu.VMEM((HEADS, ALL, 256), BF16),
            pltpu.VMEM((HEADS, ALL, 256), BF16),
            pltpu.VMEM((HEADS, ROWS, ROWS), BF16),
            pltpu.VMEM((HEADS, ROWS, ROWS), BF16),
            pltpu.VMEM((ALL, 128), F32),
            pltpu.VMEM((768, 128), F32),
            pltpu.VMEM((256, 256), F32),
            pltpu.VMEM((128, 256), F32),
            pltpu.VMEM((HEADS, ROWS, 256), F32),
            pltpu.VMEM((HEADS, ROWS, 128), BF16),
            pltpu.VMEM((HEADS, ROWS, 128), BF16),
            pltpu.VMEM((HEADS, ROWS, 256), BF16),
            pltpu.VMEM((ROWS, 256), BF16),
            pltpu.VMEM((ROWS, 256), BF16),
            pltpu.VMEM((ROWS, 512), BF16),
            pltpu.VMEM((4, ROWS, 2 * COLS), F32),
            pltpu.VMEM((8, ROWS), F32),
            pltpu.VMEM((7, 8, 256), F32),
            pltpu.VMEM((2, 4, ROWS, COLS), F32),
            pltpu.VMEM((2, 4, ROWS, COLS), BF16),
            pltpu.VMEM((2, 4, ROWS, COLS), BF16),
            pltpu.VMEM((2, ROWS, COLS), BF16),
            pltpu.VMEM((2, 2, 256, COLS), BF16),
            pltpu.VMEM((2, 2, ROWS, COLS), BF16),
            pltpu.VMEM((2, 2, ROWS, COLS), BF16),
            pltpu.SemaphoreType.DMA((9,)),
            pltpu.SemaphoreType.DMA((2, HEADS, 8)),
            pltpu.SemaphoreType.DMA((2, HEADS, 8)),
            pltpu.SemaphoreType.DMA((7,)),
            pltpu.SemaphoreType.DMA((7,)),
            pltpu.SemaphoreType.DMA((2, 10)),
            pltpu.SemaphoreType.DMA((2, 10)),
        ],
        compiler_params=pltpu.CompilerParams(
            collective_id=0, has_side_effects=True, vmem_limit_bytes=52 * 1024 * 1024 + 512 * 1024
        ),
    )(tokens, w_qkv, w_out, offsets, cotangent)
    return (both[0], both[1])


def solution(mesh):
    in_specs = (P("seq", None), P(None, None, "head"), P("head", None), P("head"), P("seq", None))
    out_specs = (P("seq", "head"), P("seq", "head"))
    return jax.shard_map(on_device, mesh=mesh, in_specs=in_specs, out_specs=out_specs, check_vma=False)
```

```python
import math

import jax
import jax.numpy as jnp
from jax import lax
from jax.experimental import pallas as pl
from jax.experimental.pallas import tpu as pltpu
from jax.sharding import PartitionSpec as P

MESH = pl.DeviceIdType.MESH
F32, BF16 = jnp.float32, jnp.bfloat16
ROWS = 512
MODEL = 2048
HD = 128
HEADS = 2
RING = 8
ALL = 1280
PAIR, QUAD0, QUAD1, OCT0, OCT1, OCT2, OCT3 = 512, 768, 896, 1024, 1088, 1152, 1216
COLS = 256
NEG = float("-inf")


def nn(a, b):
    return jnp.dot(a, b, preferred_element_type=F32)


def nt(a, b):
    return lax.dot_general(a, b, (((1,), (1,)), ((), ())), preferred_element_type=F32)


def tn(a, b):
    return lax.dot_general(a, b, (((0,), (0,)), ((), ())), preferred_element_type=F32)


def slot_table():
    tables = []
    for k in range(1, RING):
        code = 0
        for d in range(RING):
            source = (d - k) % RING
            inner = d % 4 in (1, 2)
            side = 1 if d % 2 == 1 else -1
            out_dist = (source - d) * side % RING
            in_dist = (d - source) * side % RING
            if source // 2 == d // 2:
                slot = 0
            elif source // 4 == d // 4:
                slot = 1 if source % 4 in (1, 2) else 2
            elif inner:
                slot = {2: 3, 3: 4}[in_dist] if in_dist in (2, 3) else {3: 5, 4: 6}[out_dist]
            else:
                slot = 2 + out_dist
            code += slot * 8**d
        tables.append(code)
    return tables


SLOTS = slot_table()


def kernel(
    tok_hbm, wqkv_hbm, wo_hbm, off_hbm, cot_hbm, both_ref,
    tok, wkv, wq, wo, cot, off_ref, raw, kv, qd, perm, unperm, mask_a, mask_b, mask_p, mask_q,
    grads, keep_a, keep_b, keep_c, att_p, dq_p, gkv_p, att, gq, gkv, acc, stat, stat_g,
    own, sib_out, sib_in, far, half_in, near, near_in,
    load_sem, ring_send, ring_recv, st_send, st_recv, rs_send, rs_recv, turn_sem,
):
    seq = lax.axis_index("seq")
    head = lax.axis_index("head")
    z = lax.rem(seq, RING)
    base = seq - z
    odd = lax.rem(z, 2)
    partner = (base + z + 1 - 2 * odd, head)
    outer = (base + lax.rem(z + 2 * odd + RING - 1, RING), head)
    inner = lax.rem((lax.rem(z, 4) + 1) // 2, 2) == 1
    edge = jnp.logical_not(inner)
    x, core = head // 2, lax.rem(head, 2)
    sibling = (seq, head + 1 - 2 * core)
    right = (seq, lax.rem(x + 1, 4) * 2 + core)
    left = (seq, lax.rem(x + 3, 4) * 2 + core)

    loads = [
        pltpu.make_async_copy(off_hbm, off_ref, load_sem.at[0]),
        pltpu.make_async_copy(tok_hbm, tok, load_sem.at[1]),
    ]
    for h in range(HEADS):
        for part in range(2):
            loads.append(
                pltpu.make_async_copy(
                    wqkv_hbm.at[1 + part, :, pl.ds(h * 128, 128)],
                    wkv.at[:, pl.ds(h * 256 + part * 128, 128)],
                    load_sem.at[2 + 2 * h + part],
                )
            )
    late_loads = [
        pltpu.make_async_copy(wqkv_hbm.at[0], wq, load_sem.at[6]),
        pltpu.make_async_copy(cot_hbm, cot, load_sem.at[7]),
        pltpu.make_async_copy(wo_hbm, wo, load_sem.at[8]),
    ]
    for copy in loads:
        copy.start()

    barrier = pltpu.get_barrier_semaphore()
    peers = [(base + lax.rem(z + k, RING), head) for k in range(1, RING)]
    for device in peers + [sibling, right, left]:
        pl.semaphore_signal(barrier, inc=1, device_id=device, device_id_type=MESH)

    index = lax.broadcasted_iota(jnp.int32, (ROWS, 128), 0)
    lane = lax.broadcasted_iota(jnp.int32, (ROWS, 128), 1)

    def levels(key, query, start):
        far_end = jnp.maximum(key, query)
        count = jnp.full(key.shape, float(start), F32)
        for limit in (256, 128, 64):
            count = count + jnp.where(far_end < limit, 1.0, 0.0)
        return count

    mask_a[0:512] = levels(index, lane, 1)
    mask_a[512:768] = levels(index[0:256], lane[0:256], 0)
    quad_mask = levels(index[0:128], lane[0:128], -1)
    mask_a[768:896] = quad_mask
    mask_a[896:1024] = quad_mask
    mask_a[1024:1280] = jnp.where(lane[0:256] < 64, 1.0, 0.0)
    mask_b[0:512] = levels(index, lane + 128, 1)
    mask_b[512:768] = levels(index[0:256], lane[0:256] + 128, 0)
    mask_p[:, 0:128] = levels(index[0:256], lane[0:256], 0)
    mask_p[:, 128:256] = levels(index[0:256], lane[0:256] + 128, 0)
    mask_q[:, 0:128] = quad_mask
    mask_q[:, 128:256] = quad_mask
    for copy in late_loads:
        copy.start()

    loads[0].wait()
    for h in range(HEADS):
        offset = off_ref[h]
        block = index >> 6
        turned = ((block & 1) << 2) | (block & 2) | (block >> 2)
        old = ((index & 63) << 3) + ((turned + offset) & 7)
        rest = ((index & 7) - offset) & 7
        new = ((((rest & 1) << 2) | (rest & 2) | (rest >> 2)) << 6) + (index >> 3)
        for c in range(ROWS // 128):
            perm[h, :, c * 128 : (c + 1) * 128] = jnp.where(old == lane + c * 128, 1.0, 0.0).astype(BF16)
            unperm[h, :, c * 128 : (c + 1) * 128] = jnp.where(new == lane + c * 128, 1.0, 0.0).astype(BF16)

    def remote(src, dst, send, recv, device):
        return pltpu.make_async_remote_copy(
            src_ref=src, dst_ref=dst, send_sem=send, recv_sem=recv, device_id=device, device_id_type=MESH
        )

    steps = {
        "p1": ((0, 128, PAIR), (0, 128, PAIR), partner),
        "p1b": ((128, 128, PAIR + 128), (128, 128, PAIR + 128), partner),
        "o1": ((0, 128, QUAD0), (0, 64, OCT0), outer),
        "o2": ((PAIR, 128, QUAD1), (PAIR, 64, OCT1), outer),
        "p2": ((QUAD0, 128, QUAD0), (OCT0, 64, OCT0), partner),
        "o3": ((OCT0, 64, OCT2), (QUAD0, 64, OCT2), outer),
        "p3": ((QUAD1, 128, QUAD1), (OCT1, 64, OCT1), partner),
        "o4": ((OCT1, 64, OCT3), (QUAD1, 64, OCT3), outer),
    }
    arrivals = {
        "p1": ((PAIR, 128), (PAIR, 128)),
        "p1b": ((PAIR + 128, 128), (PAIR + 128, 128)),
        "o1": ((QUAD0, 128), (OCT0, 64)),
        "o2": ((QUAD1, 128), (OCT1, 64)),
        "p2": ((OCT0, 64), (QUAD0, 128)),
        "o3": ((OCT2, 64), (OCT2, 64)),
        "p3": ((OCT1, 64), (QUAD1, 128)),
        "o4": ((OCT3, 64), (OCT3, 64)),
    }
    order = {name: i for i, name in enumerate(steps)}
    onward = {"o1": "p2", "p1": "o2", "o2": "p3", "p2": "o3", "p3": "o4"}

    class Gather:
        def __init__(self, buf, send, recv):
            self.buf, self.send_sem, self.recv_sem = buf, send, recv

        def each(self, name, act):
            in_case, edge_case, device = steps[name]
            if in_case == edge_case:
                act(in_case, device)
            else:
                pl.when(inner)(lambda: act(in_case, device))
                pl.when(edge)(lambda: act(edge_case, device))

        def copy(self, name, case, device):
            src, rows, dst = case
            i = order[name]
            return remote(
                self.buf.at[pl.ds(src, rows)], self.buf.at[pl.ds(dst, rows)],
                self.send_sem.at[i], self.recv_sem.at[i], device,
            )

        def send(self, name):
            self.each(name, lambda case, device: self.copy(name, case, device).start())

        def sent(self, name):
            self.each(name, lambda case, device: self.copy(name, case, device).wait_send())

        def arrive(self, name):
            i, device = order[name], steps[name][2]

            def act(case):
                spot = self.buf.at[pl.ds(case[0], case[1])]
                remote(spot, spot, self.send_sem.at[i], self.recv_sem.at[i], device).wait_recv()

            in_case, edge_case = arrivals[name]
            if in_case == edge_case:
                act(in_case)
            else:
                pl.when(inner)(lambda: act(in_case))
                pl.when(edge)(lambda: act(edge_case))

        def own(self):
            self.send("o1")
            self.send("p1")

        def on(self, name):
            self.arrive(name)
            self.send(onward[name])

    rings = [Gather(buf.at[h], ring_send.at[i, h], ring_recv.at[i, h]) for i, buf in enumerate((kv, qd)) for h in range(HEADS)]
    kv0, kv1, qd0, qd1 = rings

    for copy in loads[1:]:
        copy.wait()
    raw[...] = nn(tok[...], wkv[...]).astype(BF16)
    kv[0, 0:ROWS] = nn(perm[0], raw[:, 0:256]).astype(BF16)
    pl.semaphore_wait(barrier, len(peers) + 3)
    pl.when(core == 1)(lambda: pl.semaphore_wait(turn_sem, 1))
    kv0.own()
    pl.when(core == 0)(lambda: pl.semaphore_signal(turn_sem, inc=1, device_id=sibling, device_id_type=MESH))
    kv[1, 0:ROWS] = nn(perm[1], raw[:, 256:512]).astype(BF16)
    kv1.own()
    late_loads[0].wait()
    queries = (nn(tok[...], wq[...]) * (1.0 / math.sqrt(HD))).astype(BF16)
    late_loads[1].wait()
    late_loads[2].wait()
    upstream = nt(cot[...], wo[...]).astype(BF16)
    for h in range(HEADS):
        raw[:, h * 256 : h * 256 + 128] = queries[:, h * 128 : (h + 1) * 128]
        raw[:, h * 256 + 128 : h * 256 + 256] = upstream[:, h * 128 : (h + 1) * 128]
    kv0.on("p1")
    kv0.on("o1")
    pl.when(edge)(lambda: kv0.send("p1b"))
    for h in range(HEADS):
        qd[h, 0:ROWS] = nn(perm[h], raw[:, h * 256 : (h + 1) * 256]).astype(BF16)
    kv1.on("p1")
    kv1.on("o1")
    pl.when(edge)(lambda: kv1.send("p1b"))

    first, second = slice(0, 128), slice(128, 256)

    def forward(h, start, width, depth, mask, keep):
        q_rows, d_rows = qd[h, start : start + width, first], qd[h, start : start + width, second]
        s = nt(kv[h, 0:depth, first], q_rows)
        if mask is not None:
            s = jnp.where(mask[...] > 0.0, s, NEG)
        top = jnp.max(s, axis=0, keepdims=True)
        e = jnp.exp(s - top)
        if mask is not None:
            e = e * mask[...]
        inv = 1.0 / jnp.sum(e, axis=0, keepdims=True)
        p = e * inv
        if keep is not None:
            keep[...] = p
        attended = tn(p.astype(BF16), kv[h, 0:depth, second]).astype(BF16)
        att_p[h, start : start + width] = attended
        product = d_rows.astype(F32) * attended.astype(F32)
        delta = jnp.sum(product.T, axis=0, keepdims=True)
        stat[h : h + 1, start : start + width] = top
        stat[2 + h : 3 + h, start : start + width] = inv
        stat[4 + h : 5 + h, start : start + width] = delta
        return p, delta

    def backward(h, start, width, depth, p, delta, fresh):
        q_rows, d_rows = qd[h, start : start + width, first], qd[h, start : start + width, second]
        slope = (p * (nt(kv[h, 0:depth, second], d_rows) - delta)).astype(BF16)
        dq_p[h, start : start + width] = (tn(slope, kv[h, 0:depth, first]) * (1.0 / math.sqrt(HD))).astype(BF16)
        dk = nn(slope[0:ROWS], q_rows)
        dv = nn(p[0:ROWS].astype(BF16), d_rows)
        if fresh:
            grads[h, :, first] = dk
            grads[h, :, second] = dv
        else:
            grads[h, :, first] += dk
            grads[h, :, second] += dv

    def block(h, start, width, depth, mask, fresh):
        p, delta = forward(h, start, width, depth, mask, None)
        backward(h, start, width, depth, p, delta, fresh)

    forward(0, 256, 256, ROWS, None, keep_c.at[0])
    kv0.on("o2")
    forward(1, 256, 256, ROWS, None, keep_c.at[1])
    kv1.on("o2")
    kv0.on("p2")
    kv1.on("p2")

    def pair_rest(low, high):
        low.send("p1b")
        high.send("p1b")

    def query_own():
        qd0.own()
        qd1.own()

    def edge_own():
        query_own()
        pair_rest(qd0, qd1)

    pl.when(inner)(lambda: pair_rest(kv0, kv1))
    pl.when(edge)(edge_own)
    backward(0, 256, 256, ROWS, keep_c[0], stat[4:5, 256:512], True)
    kv0.on("p3")
    backward(1, 256, 256, ROWS, keep_c[1], stat[5:6, 256:512], True)
    kv1.on("p3")
    pl.when(inner)(query_own)
    kv0.arrive("p1b")
    block(0, 128, 128, 768, mask_b, False)
    kv0.arrive("o3")
    kv0.arrive("o4")

    def inner_passes(ring):
        ring.on("o1")
        ring.on("p1")

    forward(0, 0, 128, ALL, mask_a, keep_a.at[0])
    pl.when(inner)(lambda: inner_passes(qd0))
    kv1.arrive("p1b")
    forward(1, 128, 128, 768, mask_b, keep_b)
    kv1.arrive("o3")
    kv1.arrive("o4")
    pl.when(inner)(lambda: inner_passes(qd1))

    def edge_passes():
        qd0.on("p1")
        qd0.on("o1")

    pl.when(edge)(edge_passes)
    forward(1, 0, 128, ALL, mask_a, keep_a.at[1])

    st_copies = []
    for k in range(1, RING):
        spot = lax.rem(z + k, RING)
        slot = SLOTS[k - 1]
        digit = 0
        for d in range(RING):
            here = 1 - (spot - d) * (spot - d)
            here = (here + jnp.abs(here)) // 2
            digit = digit + here * (slot // 8**d % 8)
        copy = remote(
            stat.at[:, pl.ds(0, 256)], stat_g.at[digit], st_send.at[k - 1], st_recv.at[k - 1], peers[k - 1]
        )
        copy.start()
        st_copies.append(copy)

    pl.when(inner)(lambda: qd0.on("o2"))
    pl.when(edge)(lambda: qd1.on("o1"))

    class Scatter:
        def __init__(self, r):
            self.r = r
            self.copies = []

        def sems(self, i):
            return rs_send.at[self.r, i], rs_recv.at[self.r, i]

        def send(self, i, src, dst, device):
            copy = remote(src, dst, *self.sems(i), device)
            copy.start()
            self.copies.append((src, dst, i, device))

        def arrive(self, i, dst, device):
            remote(dst, dst, *self.sems(i), device).wait_recv()

        def part(self, dx, product):
            r = self.r
            both = product(dx)
            low, high = both[:, 0:COLS], both[:, COLS : 2 * COLS]
            sib_out[r, dx] = jnp.where(core == 0, high, low).astype(BF16)
            self.send(dx, sib_out.at[r, dx], sib_in.at[r, dx], sibling)
            own[r, dx] = jnp.where(core == 0, low, high)

        def pair_sum(self, dx):
            r = self.r
            self.arrive(dx, sib_in.at[r, dx], sibling)
            return own[r, dx] + sib_in[r, dx].astype(F32)

        def halves(self):
            r = self.r
            far[r] = self.pair_sum(2).astype(BF16)
            for i, device in ((0, right), (1, left)):
                remote(far.at[r, pl.ds(i * 256, 256)], half_in.at[r, i], *self.sems(4 + i), device).start()

        def direct(self):
            r = self.r
            own[r, 1] = self.pair_sum(1)
            near[r, 0, 256:512] = own[r, 1, 256:512].astype(BF16)
            self.send(6, near.at[r, 0, pl.ds(256, 256)], near_in.at[r, 0, pl.ds(256, 256)], right)
            own[r, 3] = self.pair_sum(3)
            near[r, 1, 0:256] = own[r, 3, 0:256].astype(BF16)
            self.send(7, near.at[r, 1, pl.ds(0, 256)], near_in.at[r, 1, pl.ds(0, 256)], left)

        def summed(self):
            r = self.r
            self.arrive(4, half_in.at[r, 0], right)
            near[r, 0, 0:256] = (own[r, 1, 0:256] + half_in[r, 0].astype(F32)).astype(BF16)
            self.send(8, near.at[r, 0, pl.ds(0, 256)], near_in.at[r, 0, pl.ds(0, 256)], right)
            self.arrive(5, half_in.at[r, 1], left)
            near[r, 1, 256:512] = (own[r, 3, 256:512] + half_in[r, 1].astype(F32)).astype(BF16)
            self.send(9, near.at[r, 1, pl.ds(256, 256)], near_in.at[r, 1, pl.ds(256, 256)], left)

        def last(self, into):
            r = self.r
            mine = self.pair_sum(0)
            self.arrive(6, near_in.at[r, 0, pl.ds(256, 256)], right)
            self.arrive(7, near_in.at[r, 1, pl.ds(0, 256)], left)
            self.arrive(8, near_in.at[r, 0, pl.ds(0, 256)], right)
            self.arrive(9, near_in.at[r, 1, pl.ds(256, 256)], left)
            into[...] = (mine + near_in[r, 0].astype(F32) + near_in[r, 1].astype(F32)).astype(BF16)

        def drain(self):
            for src, dst, i, device in self.copies:
                remote(src, dst, *self.sems(i), device).wait_send()
            for i, device in ((0, right), (1, left)):
                remote(
                    far.at[self.r, pl.ds(i * 256, 256)], half_in.at[self.r, i], *self.sems(4 + i), device
                ).wait_send()

    def chip_span(dx):
        return pl.ds(pl.multiple_of(lax.rem(x + dx, 4) * 2 * COLS, 2 * COLS), 2 * COLS)

    for h in range(HEADS):
        att[:, h * 128 : (h + 1) * 128] = nn(unperm[h], att_p[h]).astype(BF16)
    scatter_out = Scatter(0)

    def forward_part(dx):
        scatter_out.part(dx, lambda dx: nn(att[...], wo[:, chip_span(dx)]))

    forward_part(2)
    pl.when(core == 0)(scatter_out.halves)
    pl.when(edge)(lambda: qd1.on("p1"))
    forward_part(1)

    def inner_more():
        qd1.on("o2")
        pair_rest(qd0, qd1)

    pl.when(inner)(inner_more)
    forward_part(3)
    forward_part(0)
    pl.when(core == 1)(scatter_out.halves)
    qd0.on("p2")
    backward(1, 128, 128, 768, keep_b[...], stat[5:6, 128:256], False)
    pl.when(edge)(lambda: qd0.on("o2"))
    backward(0, 0, 128, ALL, keep_a[0], stat[4:5, 0:128], False)
    qd1.on("p2")
    pl.when(edge)(lambda: qd1.on("o2"))
    backward(1, 0, 128, ALL, keep_a[1], stat[5:6, 0:128], False)
    scatter_out.direct()
    qd0.on("p3")
    for k in range(1, RING):
        remote(
            stat_g.at[0], stat_g.at[0], st_send.at[k - 1], st_recv.at[k - 1], peers[k - 1]
        ).wait_recv()
    quad_stat = jnp.concatenate([stat_g[1, :, 0:128], stat_g[2, :, 0:128]], 1)
    low_lanes = lax.broadcasted_iota(jnp.int32, (8, 128), 1) < 64
    oct_stat = jnp.concatenate(
        [
            jnp.where(low_lanes, stat_g[a, :, 0:128], pltpu.roll(stat_g[a + 1, :, 0:128], 64, 1))
            for a in (3, 5)
        ],
        1,
    )

    def far_block(h, start, depth, stats, mask):
        q_rows, d_rows = qd[h, start : start + 256, first], qd[h, start : start + 256, second]
        top, inv, delta = (stats[i : i + 1] for i in (h, 2 + h, 4 + h))
        p = jnp.exp(nt(kv[h, 0:depth, first], q_rows) - top) * inv
        if mask is not None:
            p = p * mask[...]
        p_low = p.astype(BF16)
        slope = (p * (nt(kv[h, 0:depth, second], d_rows) - delta)).astype(BF16)
        grads[h, 0:depth, first] += nn(slope, q_rows)
        grads[h, 0:depth, second] += nn(p_low, d_rows)

    def to_tokens(h):
        gkv_p[h] = grads[h].astype(BF16)
        gkv[:, h * 256 : (h + 1) * 256] = nn(unperm[h], gkv_p[h]).astype(BF16)

    far_block(0, QUAD0, 128, quad_stat, mask_q)
    for h in range(HEADS):
        gq[:, h * 128 : (h + 1) * 128] = nn(unperm[h], dq_p[h]).astype(BF16)
    qd1.on("p3")
    for dx in (2, 1, 3, 0):
        acc[dx] = nt(gq[...], wq[chip_span(dx)])
    far_block(1, QUAD0, 128, quad_stat, mask_q)
    qd0.arrive("p1b")
    far_block(0, PAIR, 256, stat_g[0], mask_p)
    scatter_out.summed()
    qd0.arrive("o3")
    qd0.arrive("o4")
    far_block(0, OCT0, 64, oct_stat, None)
    to_tokens(0)
    qd1.arrive("p1b")
    far_block(1, PAIR, 256, stat_g[0], mask_p)
    qd1.arrive("o3")
    qd1.arrive("o4")
    far_block(1, OCT0, 64, oct_stat, None)
    to_tokens(1)

    scatter_in = Scatter(1)

    def back(dx):
        return acc[dx] + nt(gkv[...], wkv[chip_span(dx)])

    scatter_in.part(2, back)
    pl.when(core == 0)(scatter_in.halves)
    scatter_in.part(1, back)
    scatter_in.part(3, back)
    pl.when(core == 1)(scatter_in.halves)
    scatter_in.direct()
    scatter_in.part(0, back)
    scatter_out.last(both_ref.at[0])
    scatter_in.summed()
    scatter_in.last(both_ref.at[1])

    for name in steps:
        for ring in rings:
            ring.sent(name)
    for copy in st_copies:
        copy.wait_send()
    scatter_out.drain()
    scatter_in.drain()


def on_device(tokens, w_qkv, w_out, offsets, cotangent):
    whole = pl.BlockSpec(memory_space=pl.ANY)
    vmem = pl.BlockSpec(memory_space=pltpu.VMEM)
    both = pl.pallas_call(
        kernel,
        out_shape=jax.ShapeDtypeStruct((2, ROWS, COLS), BF16),
        in_specs=[whole] * 5,
        out_specs=vmem,
        scratch_shapes=[
            pltpu.VMEM((ROWS, MODEL), BF16),
            pltpu.VMEM((MODEL, 512), BF16),
            pltpu.VMEM((MODEL, 256), BF16),
            pltpu.VMEM((256, MODEL), BF16),
            pltpu.VMEM((ROWS, MODEL), BF16),
            pltpu.SMEM((HEADS,), jnp.int32),
            pltpu.VMEM((ROWS, 512), BF16),
            pltpu.VMEM((HEADS, ALL, 256), BF16),
            pltpu.VMEM((HEADS, ALL, 256), BF16),
            pltpu.VMEM((HEADS, ROWS, ROWS), BF16),
            pltpu.VMEM((HEADS, ROWS, ROWS), BF16),
            pltpu.VMEM((ALL, 128), F32),
            pltpu.VMEM((768, 128), F32),
            pltpu.VMEM((256, 256), F32),
            pltpu.VMEM((128, 256), F32),
            pltpu.VMEM((HEADS, ROWS, 256), F32),
            pltpu.VMEM((HEADS, ALL, 128), F32),
            pltpu.VMEM((768, 128), F32),
            pltpu.VMEM((HEADS, ROWS, 256), F32),
            pltpu.VMEM((HEADS, ROWS, 128), BF16),
            pltpu.VMEM((HEADS, ROWS, 128), BF16),
            pltpu.VMEM((HEADS, ROWS, 256), BF16),
            pltpu.VMEM((ROWS, 256), BF16),
            pltpu.VMEM((ROWS, 256), BF16),
            pltpu.VMEM((ROWS, 512), BF16),
            pltpu.VMEM((4, ROWS, 2 * COLS), F32),
            pltpu.VMEM((8, ROWS), F32),
            pltpu.VMEM((7, 8, 256), F32),
            pltpu.VMEM((2, 4, ROWS, COLS), F32),
            pltpu.VMEM((2, 4, ROWS, COLS), BF16),
            pltpu.VMEM((2, 4, ROWS, COLS), BF16),
            pltpu.VMEM((2, ROWS, COLS), BF16),
            pltpu.VMEM((2, 2, 256, COLS), BF16),
            pltpu.VMEM((2, 2, ROWS, COLS), BF16),
            pltpu.VMEM((2, 2, ROWS, COLS), BF16),
            pltpu.SemaphoreType.DMA((9,)),
            pltpu.SemaphoreType.DMA((2, HEADS, 8)),
            pltpu.SemaphoreType.DMA((2, HEADS, 8)),
            pltpu.SemaphoreType.DMA((7,)),
            pltpu.SemaphoreType.DMA((7,)),
            pltpu.SemaphoreType.DMA((2, 10)),
            pltpu.SemaphoreType.DMA((2, 10)),
            pltpu.SemaphoreType.REGULAR,
        ],
        compiler_params=pltpu.CompilerParams(
            collective_id=0, has_side_effects=True, vmem_limit_bytes=52 * 1024 * 1024 + 512 * 1024
        ),
    )(tokens, w_qkv, w_out, offsets, cotangent)
    return (both[0], both[1])


def solution(mesh):
    in_specs = (P("seq", None), P(None, None, "head"), P("head", None), P("head"), P("seq", None))
    out_specs = (P("seq", "head"), P("seq", "head"))
    return jax.shard_map(on_device, mesh=mesh, in_specs=in_specs, out_specs=out_specs, check_vma=False)
```
